128 devices in a mesh: row: 8 (over y, core), col: 16 (over x, z).
Axes of the slice: x: 4, y: 4, z: 4, core: 2. Of those that a mesh axis runs over, the one named last changes fastest.
Arguments:
- forcing: bfloat16 [8, 1048576], P(None, ('row', 'col')), may hold values from 0 to 1
- owner: int32 [1048576], P(('row', 'col')), may hold values from 0 to 127, as said below
- column: int32 [1048576], P(('row', 'col')), may hold values from 0 to 127
- area: float32 [1048576], P(('row', 'col')), may hold values from 0.25 to 2
- sunlit: int32 [1048576], P(('row', 'col')), may hold values 0 or 1
- plant_type: int32 [1048576], P(('row', 'col')), may hold values from 0 to 15
- leaf_area: float32 [1048576], P(('row', 'col')), may hold values from 0.5 to 6
- soil_water: float32 [15, 1048576], P(None, ('row', 'col')), may hold values from 0.1 to 0.4
- pft_table: float32 [4, 16], replicated, may hold values from 0 to 1
Outputs:
- atm_flux: float32 [4, 262144], P(None, ('row', 'col'))
- soil_after: float32 [15, 1048576], P(None, ('row', 'col'))
The draws below stay inside these ranges and needn't reach their ends.
Inputs may be any that keep to these rules, and one draw needn't show every extreme that they name: Every device owns exactly 8192 rows; the rows of one device name one owner at most 80 times, and exactly 80 times for some device and owner in every draw.
All inputs are finite; a program needn't handle non-finite values. No bound on the sum of `sunlit` on one device may be relied on, other than what follows from the above.
Results may differ from the reference program's by a relative error of at most 0.0018.
Values may be sent and summed in bfloat16 or wider, within the bound.
A program may use at most 64 MiB of HBM per device.

```python
import math
import jax
import jax.numpy as jnp
from jax import lax

ROWS_DEV = 8192
NF = 8
NOUT = 4
NPFT = 16
NPAR = 4
LEVELS = 15
ITERS = 4
SOILP = 4
BROWS = 512
BCOLS = 128
ROWS = 1048576
COLS = 262144
DEVICES = 128


def draw_owner(key, part):
    key = jax.random.fold_in(key, 7)
    key_sigma, key_tau, key_first, key_second, key_rows = jax.random.split(key, 5)
    peers = DEVICES
    mean_rows = ROWS_DEV // DEVICES
    quarter = ROWS_DEV // (4 * DEVICES)
    sigma = jax.random.permutation(key_sigma, peers)
    tau = jax.random.permutation(key_tau, peers)
    quads = peers // 4
    first = jax.random.randint(key_first, (quads,), -quarter, quarter + 1)
    first = first.at[0].set(quarter)
    second = jax.random.randint(key_second, (quads,), -quarter, quarter + 1)
    pattern = jnp.stack([first, second, -first, -second], axis=1).reshape(peers)
    parity = 1 - 2 * (tau % 2)
    weights = mean_rows + parity[:, None] * pattern[None, :]
    offsets = jnp.arange(peers)
    targets = sigma[(tau[:, None] + offsets[None, :]) % peers]
    bounds = jnp.cumsum(weights, axis=1)
    ranks = jnp.arange(ROWS_DEV)

    def one_source(source_key, bound_row, target_row):
        shuffle = jax.random.permutation(source_key, ROWS_DEV)
        segment = jnp.searchsorted(bound_row, ranks, side='right')
        segment = jnp.minimum(segment, peers - 1)
        return jnp.zeros((ROWS_DEV,), jnp.int32).at[shuffle].set(target_row[segment].astype(jnp.int32))
    blocks = jax.vmap(one_source)(jax.random.split(key_rows, peers), bounds, targets)
    return blocks.reshape(ROWS_DEV * peers).astype(jnp.int32)


def set_ends(result, stream_key, least, top_value):
    dims = result.shape
    index_at = [jax.random.randint(jax.random.fold_in(stream_key, axis), (), 0, dims[axis]) for axis in range(len(dims))]
    result = result.at[tuple(index_at)].set(least)
    longest = dims.index(max(dims))
    index_at[longest] = (index_at[longest] + 1) % dims[longest]
    return result.at[tuple(index_at)].set(top_value)


def level_of(rng, extent, pieces, smallest, largest):
    def one(position, shards_of):
        draws = jax.random.uniform(jax.random.fold_in(jax.random.fold_in(rng, 6), position), (shards_of,), jnp.float32, smallest / len(pieces), largest / len(pieces))
        return jnp.repeat(jnp.exp(draws), extent[position] // shards_of).reshape((-1,) + (1,) * (len(extent) - position - 1))

    factor_of = one(*pieces[0])
    for cut in pieces[1:]:
        factor_of = factor_of * one(*cut)
    return factor_of


def setup_inputs(seed: int = 0) -> dict:
    key_list = jax.random.split(jax.random.key(seed), 10)
    return {
        "forcing": jnp.clip(1.0 * jax.random.uniform(key_list[0], (NF, ROWS), jnp.float32) ** level_of(key_list[0], (NF, ROWS), ((1, 128),), -0.2, 0.2), 0.0, 1.0).astype(jnp.bfloat16),
        "owner": draw_owner(jax.random.fold_in(key_list[9], 71), 0),
        "column": set_ends(jax.random.randint(key_list[2], (ROWS,), 0, BCOLS), jax.random.fold_in(key_list[2], 1), 0, BCOLS - 1).astype(jnp.int32),
        "area": jnp.clip(jnp.exp(math.log(2.0) - 2.0794415 * jax.random.uniform(key_list[3], (ROWS,), jnp.float32) ** level_of(key_list[3], (ROWS,), ((0, 128),), -0.2, 0.2)), 0.25, 2.0),
        "sunlit": set_ends((jax.random.randint(key_list[4], (ROWS,), 0, 2) < 1).astype(jnp.int32), jax.random.fold_in(key_list[4], 1), 0, 1),
        "plant_type": set_ends(jax.random.randint(key_list[5], (ROWS,), 0, NPFT), jax.random.fold_in(key_list[5], 1), 0, NPFT - 1).astype(jnp.int32),
        "leaf_area": jnp.clip(jnp.exp(math.log(6.0) - 2.4849066 * jax.random.uniform(key_list[6], (ROWS,), jnp.float32) ** level_of(key_list[6], (ROWS,), ((0, 128),), -0.2, 0.2)), 0.5, 6.0),
        "soil_water": jnp.clip(0.1 + 0.3 * jax.random.uniform(key_list[7], (LEVELS, ROWS), jnp.float32) ** level_of(key_list[7], (LEVELS, ROWS), ((1, 128),), -0.2, 0.2), 0.1, 0.4),
        "pft_table": jnp.clip(jax.random.uniform(key_list[8], (NPAR, NPFT), jnp.float32, 0.0, 1.0), 0.0, 1.0),
    }


def land_physics(fields, sunlit_f, params, leaf_area, theta):
    omega = 0.1 + 0.3 * params[0]
    vcmax = 0.5 + 1.5 * params[1]
    slope = 3.0 + 6.0 * params[2]
    kroot = 0.05 + 0.5 * params[3]
    swdir = 2.0 * fields[0]
    swdif = fields[1]
    tair = fields[2] - 0.5
    vapour = 0.2 + fields[3]
    carbon = 0.8 + 0.4 * fields[4]
    coszen = 0.1 + 0.9 * fields[5]
    wind_speed = 0.5 + 2.0 * fields[6]
    precip = fields[7]
    single = jnp.sqrt(1.0 - omega)
    extinct = 0.5 / coszen
    reflect_h = (1.0 - single) / (1.0 + single)
    reflect_b = 2.0 * extinct * reflect_h / (1.0 + extinct)
    light = sunlit_f * ((1.0 - reflect_b) * swdir * (1.0 - jnp.exp(-extinct * single * leaf_area)) + (1.0 - reflect_h) * swdif * (1.0 - jnp.exp(-0.8 * single * leaf_area)))
    electrons = 0.3 * light
    compensation = 0.08 * (1.0 + 0.3 * tair)
    capacity_t = vcmax * jnp.exp(0.5 * tair)
    internal = 0.7 * carbon
    assim = jnp.zeros_like(internal)
    conduct = jnp.zeros_like(internal)
    for repeat in range(ITERS):
        limit = internal - compensation
        carboxyl = capacity_t * limit / (internal + 0.6)
        ribulose = electrons * limit / (4.0 * internal + 8.0 * compensation)
        assim = carboxyl * ribulose / (carboxyl + ribulose)
        conduct = 0.05 + slope * assim / carbon
        internal = carbon - 1.6 * assim / conduct
    transpire = conduct * vapour
    sensible = 0.5 * wind_speed * (0.2 * light - 0.5 * transpire)
    depths = jnp.arange(LEVELS, dtype=jnp.float32)
    roots = jnp.exp(-kroot[None, :] * depths[:, None])
    roots = roots / lax.optimization_barrier(jnp.sum(roots, axis=0, keepdims=True))
    theta = jnp.concatenate([theta[:1] + 0.1 * precip[None, :], theta[1:]], axis=0)
    for repeat in range(SOILP):
        above = jnp.concatenate([theta[:1], theta[:-1]], axis=0)
        below = jnp.concatenate([theta[1:], theta[-1:]], axis=0)
        theta = theta + 0.25 * (above + below - 2.0 * theta) - 0.05 * transpire[None, :] * roots
    drainage = 0.5 * theta[LEVELS - 1]
    tile_flux = jnp.stack([assim, transpire, sensible, drainage], axis=0).astype(jnp.bfloat16)
    return (tile_flux, theta)

def reference(forcing, owner, column, area, sunlit, plant_type, leaf_area, soil_water, pft_table):
    order = jnp.argsort(owner, stable=True).astype(jnp.int32)
    fields = forcing[:, order].astype(jnp.float32)
    params = pft_table[:, plant_type]
    tile_flux, soil_after = land_physics(fields, sunlit.astype(jnp.float32), params, leaf_area, soil_water)
    row_flux = jnp.zeros((NOUT, ROWS), jnp.float32).at[:, order].set(tile_flux.astype(jnp.float32))
    weighted = row_flux * area[None, :]
    segment = jnp.arange(ROWS, dtype=jnp.int32) // BROWS * BCOLS + column
    atm_flux = jax.ops.segment_sum(weighted.T, segment, num_segments=COLS).T
    return (atm_flux, soil_after)
```

```python
import functools

import jax
import jax.numpy as jnp
from jax import lax
from jax.experimental import pallas as pl
from jax.experimental.pallas import tpu as pltpu
from jax.sharding import PartitionSpec as P

NF = 8
NOUT = 4
NPFT = 16
LEVELS = 15
ITERS = 4
SOILP = 4
BROWS = 512
BCOLS = 128
PEERS = 128
ROWS = 8192
LINES = ROWS // 128
SLOTS = 80
STEP = 256
WIDE = 1024
MESH = pl.DeviceIdType.MESH
F32 = jnp.float32
BF16 = jnp.bfloat16
NT = (((1,), (1,)), ((), ()))


def iota(shape, dim):
    return lax.broadcasted_iota(jnp.int32, shape, dim)


def as_bf16(mask):
    return jnp.where(mask, 1.0, 0.0).astype(BF16)


def dot(a, b):
    return jnp.dot(a, b, preferred_element_type=F32)


def dot_nt(a, b):
    return lax.dot_general(a, b, NT, preferred_element_type=F32)


def spread(hot, row):
    width = row.shape[1]
    tile = jnp.broadcast_to(row, (16, width)).astype(BF16)
    parts = hot.reshape(SLOTS // 16, 16, width) * tile[None]
    return parts.reshape(SLOTS, width)


def pack_kernel(owner_ref, forcing_ref, msg_ref, rank_ref, at_ref, w_ref, acc_ref):
    ids = iota((PEERS, 128), 0)
    for j in range(LINES):
        at_ref[:, 128 * j : 128 * j + 128] = as_bf16(ids == owner_ref[j : j + 1, :])
    base = jnp.zeros((PEERS, 128), F32)
    for g in range(ROWS // WIDE):
        earlier = as_bf16((iota((WIDE, 128), 0) + g * WIDE) // STEP < iota((WIDE, 128), 1))
        base = base + dot(at_ref[:, g * WIDE : (g + 1) * WIDE], earlier)
    upper = as_bf16(iota((STEP, STEP), 0) < iota((STEP, STEP), 1))
    slot = iota((SLOTS, STEP), 0).astype(F32)
    w_ref[NF * SLOTS :, :] = jnp.ones((16, WIDE), BF16)
    for g in range(ROWS // WIDE):
        for k in range(WIDE // STEP):
            c = g * (WIDE // STEP) + k
            a = at_ref[:, c * STEP : (c + 1) * STEP]
            seen = dot(a, upper) + base[:, c : c + 1]
            rank = jnp.sum(a.astype(F32) * seen, axis=0, keepdims=True)
            rank_ref[2 * c : 2 * c + 1, :] = rank[:, :128]
            rank_ref[2 * c + 1 : 2 * c + 2, :] = rank[:, 128:]
            hot = as_bf16(slot == rank)
            x = forcing_ref[:, c * STEP : (c + 1) * STEP].astype(F32)
            for f in range(NF):
                w_ref[f * SLOTS : (f + 1) * SLOTS, k * STEP : (k + 1) * STEP] = spread(hot, x[f : f + 1, :])
        part = dot_nt(w_ref[...], at_ref[:, g * WIDE : (g + 1) * WIDE])
        if g == 0:
            acc_ref[...] = part
        else:
            acc_ref[...] += part
    counts = acc_ref[NF * SLOTS : NF * SLOTS + 1, :]
    held = iota((SLOTS, PEERS), 0).astype(F32) < counts
    acc_ref[:SLOTS, :] = jnp.where(held, acc_ref[:SLOTS, :], -1.0)
    for i in range(NF * SLOTS // 128):
        msg_ref[pl.ds(i, PEERS, stride=8), :] = acc_ref[128 * i : 128 * (i + 1), :].T


def exchange_kernel(lines, cols, in_ref, out_ref, send_sem, recv_sem):
    me = lax.axis_index("row") * cols + lax.axis_index("col")
    barrier = pltpu.get_barrier_semaphore()

    def place(p):
        to = lax.rem(me + p, PEERS)
        return to, (to // cols, lax.rem(to, cols))

    def greet(p, carry):
        pl.semaphore_signal(barrier, inc=1, device_id=place(p)[1], device_id_type=MESH)
        return carry

    lax.fori_loop(1, PEERS, greet, 0)
    pl.semaphore_wait(barrier, PEERS - 1)
    own = pltpu.make_async_copy(in_ref.at[me, :lines], out_ref.at[me, :lines], recv_sem)
    own.start()

    def send(p, carry):
        to, device = place(p)
        pltpu.make_async_remote_copy(
            src_ref=in_ref.at[to, :lines],
            dst_ref=out_ref.at[me, :lines],
            send_sem=send_sem,
            recv_sem=recv_sem,
            device_id=device,
            device_id_type=MESH,
        ).start()
        return carry

    lax.fori_loop(1, PEERS, send, 0)
    sent = in_ref.at[: PEERS - 1, :lines]
    pltpu.make_async_copy(sent, sent, send_sem).wait()
    got = out_ref.at[:, :lines]
    pltpu.make_async_copy(got, got, recv_sem).wait()


def exchange(message, lines, cols, ident):
    return pl.pallas_call(
        functools.partial(exchange_kernel, lines, cols),
        out_shape=jax.ShapeDtypeStruct((PEERS, 8, 128), F32),
        in_specs=[pl.BlockSpec(memory_space=pl.ANY)],
        out_specs=pl.BlockSpec(memory_space=pl.ANY),
        scratch_shapes=[pltpu.SemaphoreType.DMA, pltpu.SemaphoreType.DMA],
        compiler_params=pltpu.CompilerParams(collective_id=ident, has_side_effects=True),
    )(message.reshape(PEERS, 8, 128)).reshape(PEERS * 8, 128)


def unfold(recv_ref, out_ref, lines):
    for i in range(lines):
        out_ref[128 * i : 128 * (i + 1), :] = recv_ref[pl.ds(i, PEERS, stride=8), :].T


def land_kernel(
    recv_ref, sunlit_ref, type_ref, leaf_ref, soil_ref, table_ref,
    msg_ref, after_ref,
    got_ref, p_ref, q_ref, field_ref, flux_ref, w_ref, acc_ref,
):
    unfold(recv_ref, acc_ref, NF * SLOTS // 128)
    counts = jnp.sum(jnp.where(acc_ref[:SLOTS, :] >= 0.0, 1.0, 0.0), axis=0, keepdims=True)
    below = iota((PEERS, PEERS), 1) < iota((PEERS, PEERS), 0)
    upto = iota((PEERS, PEERS), 1) <= iota((PEERS, PEERS), 0)
    after = as_bf16(iota((PEERS, PEERS), 0) < iota((PEERS, PEERS), 1))
    ones = jnp.ones((PEERS, STEP), BF16)
    begin = dot(jnp.where(below, counts, 0.0).astype(BF16), ones)
    end = dot(jnp.where(upto, counts, 0.0).astype(BF16), ones)
    begin_row = dot(jnp.broadcast_to(counts, (16, PEERS)).astype(BF16), after)
    high = jnp.floor(begin_row * (1.0 / 128.0))
    line = iota((16, PEERS), 0)
    tail = jnp.where(line == 0, high, jnp.where(line == 1, begin_row - 128.0 * high, 0.0))
    got_ref[: NF * SLOTS, :] = acc_ref[...].astype(BF16)
    got_ref[NF * SLOTS :, :] = tail.astype(BF16)
    slot = iota((SLOTS, STEP), 0).astype(F32)
    lane = iota((PEERS, STEP), 1).astype(F32)
    for c in range(ROWS // STEP):
        tile = lane + float(c * STEP)
        p = as_bf16((tile >= begin) & (tile < end))
        p_ref[:, c * STEP : (c + 1) * STEP] = p
        g = dot(got_ref[...], p)
        place = tile[:1, :] - (128.0 * g[NF * SLOTS : NF * SLOTS + 1, :] + g[NF * SLOTS + 1 : NF * SLOTS + 2, :])
        q = slot == place
        q_ref[:, c * STEP : (c + 1) * STEP] = as_bf16(q)
        for f in range(NF):
            value = jnp.sum(jnp.where(q, g[f * SLOTS : (f + 1) * SLOTS, :], 0.0), axis=0, keepdims=True)
            field_ref[f, 2 * c : 2 * c + 1, :] = value[:, :128]
            field_ref[f, 2 * c + 1 : 2 * c + 2, :] = value[:, 128:]

    table = jnp.concatenate([table_ref[...], jnp.zeros((4, 128 - NPFT), F32)], axis=1)
    single_t = jnp.sqrt(1.0 - (0.1 + 0.3 * table[0:1]))
    reflect_t = (1.0 - single_t) / (1.0 + single_t)
    vcmax_t = 0.5 + 1.5 * table[1:2]
    slope_t = 3.0 + 6.0 * table[2:3]
    kroot_t = 0.05 + 0.5 * table[3:4]
    level = iota((16, 128), 0)
    roots_t = jnp.where(level < LEVELS, jnp.exp(-kroot_t * level.astype(F32)), 0.0)
    roots_t = 0.05 * (roots_t / jnp.sum(roots_t, axis=0, keepdims=True))
    kinds = type_ref[...]

    def look(row):
        return jnp.take_along_axis(jnp.broadcast_to(row, (LINES, 128)), kinds, axis=1, mode="promise_in_bounds")

    single = look(single_t)
    reflect_h = look(reflect_t)
    vcmax = look(vcmax_t)
    slope = look(slope_t)
    leaf = leaf_ref[...]
    swdir = 2.0 * field_ref[0]
    swdif = field_ref[1]
    tair = field_ref[2] - 0.5
    vapour = 0.2 + field_ref[3]
    carbon = 0.8 + 0.4 * field_ref[4]
    coszen = 0.1 + 0.9 * field_ref[5]
    wind_speed = 0.5 + 2.0 * field_ref[6]
    extinct = 0.5 / coszen
    reflect_b = 2.0 * extinct * reflect_h / (1.0 + extinct)
    light = sunlit_ref[...].astype(F32) * (
        (1.0 - reflect_b) * swdir * (1.0 - jnp.exp(-extinct * single * leaf))
        + (1.0 - reflect_h) * swdif * (1.0 - jnp.exp(-0.8 * single * leaf))
    )
    electrons = 0.3 * light
    compensation = 0.08 * (1.0 + 0.3 * tair)
    capacity_t = vcmax * jnp.exp(0.5 * tair)
    internal = 0.7 * carbon
    for repeat in range(ITERS):
        limit = internal - compensation
        carboxyl = capacity_t * limit / (internal + 0.6)
        ribulose = electrons * limit / (4.0 * internal + 8.0 * compensation)
        assim = carboxyl * ribulose / (carboxyl + ribulose)
        conduct = 0.05 + slope * assim / carbon
        internal = carbon - 1.6 * assim / conduct
    transpire = conduct * vapour
    flux_ref[0] = assim
    flux_ref[1] = transpire
    flux_ref[2] = 0.5 * wind_speed * (0.2 * light - 0.5 * transpire)

    top = iota((16, 128), 0) == 0
    for j in range(LINES):
        kind = jnp.broadcast_to(type_ref[j : j + 1, :], (16, 128))
        draw = jnp.take_along_axis(roots_t, kind, axis=1, mode="promise_in_bounds")
        draw = (draw * flux_ref[1, j : j + 1, :])[:LEVELS]
        theta = soil_ref[:, 128 * j : 128 * (j + 1)]
        theta = theta + jnp.where(top, 0.1 * field_ref[7, j : j + 1, :], 0.0)[:LEVELS]
        for repeat in range(SOILP):
            above = jnp.concatenate([theta[:1], theta[:-1]], axis=0)
            under = jnp.concatenate([theta[1:], theta[-1:]], axis=0)
            theta = theta + 0.25 * (above + under - 2.0 * theta) - draw
        after_ref[:, 128 * j : 128 * (j + 1)] = theta
        flux_ref[3, j : j + 1, :] = 0.5 * theta[LEVELS - 1 :, :]

    for g in range(ROWS // WIDE):
        for k in range(WIDE // 128):
            j = g * (WIDE // 128) + k
            hot = q_ref[:, 128 * j : 128 * (j + 1)]
            for f in range(NOUT):
                w_ref[f * SLOTS : (f + 1) * SLOTS, 128 * k : 128 * (k + 1)] = spread(hot, flux_ref[f, j : j + 1, :])
        part = dot_nt(w_ref[...], p_ref[:, g * WIDE : (g + 1) * WIDE])
        if g == 0:
            acc_ref[: NOUT * SLOTS, :] = part
        else:
            acc_ref[: NOUT * SLOTS, :] += part
    for i in range(3):
        msg_ref[pl.ds(i, PEERS, stride=8), :] = acc_ref[128 * i : 128 * (i + 1), :].T


def gather_kernel(recv_ref, owner_ref, rank_ref, area_ref, column_ref, atm_ref, acc_ref):
    unfold(recv_ref, acc_ref, 3)
    got = acc_ref[: NOUT * SLOTS, :].astype(BF16)
    ids = iota((PEERS, 128), 0)
    slot = iota((SLOTS, 128), 0).astype(F32)
    for b in range(ROWS // BROWS):
        weights, targets = [], []
        for k in range(BROWS // STEP):
            c = b * (BROWS // STEP) + k
            a = jnp.concatenate(
                [as_bf16(ids == owner_ref[j : j + 1, :]) for j in (2 * c, 2 * c + 1)], axis=1
            )
            g = dot(got, a)
            q = jnp.concatenate([slot == rank_ref[j : j + 1, :] for j in (2 * c, 2 * c + 1)], axis=1)
            scale = jnp.concatenate([area_ref[j : j + 1, :] for j in (2 * c, 2 * c + 1)], axis=1)
            rows = [
                jnp.sum(jnp.where(q, g[f * SLOTS : (f + 1) * SLOTS, :], 0.0), axis=0, keepdims=True) * scale
                for f in range(NOUT)
            ]
            weights.append(jnp.concatenate(rows, axis=0))
            targets += [as_bf16(ids == column_ref[j : j + 1, :]) for j in (2 * c, 2 * c + 1)]
        weight = jnp.concatenate(weights, axis=1)
        high = weight.astype(BF16).astype(F32)
        both = jnp.concatenate([high, weight - high], axis=0).astype(BF16)
        total = dot_nt(both, jnp.concatenate(targets, axis=1))
        atm_ref[:, BCOLS * b : BCOLS * (b + 1)] = total[:NOUT] + total[NOUT:]


VMEM_LIMIT = 48 * 1024 * 1024


def local_call(kernel, outs, scratch, name):
    return pl.pallas_call(
        kernel,
        out_shape=outs,
        scratch_shapes=scratch,
        compiler_params=pltpu.CompilerParams(vmem_limit_bytes=VMEM_LIMIT),
        name=name,
    )


def shape(dims, dtype=F32):
    return jax.ShapeDtypeStruct(dims, dtype)


def body(cols, forcing, owner, column, area, sunlit, plant_type, leaf_area, soil_water, pft_table):
    lines = lambda x: x.reshape(LINES, 128)
    owner = lines(owner)
    message, rank = local_call(
        pack_kernel,
        (shape((PEERS * 8, 128)), shape((LINES, 128))),
        [
            pltpu.VMEM((PEERS, ROWS), BF16),
            pltpu.VMEM((NF * SLOTS + 16, WIDE), BF16),
            pltpu.VMEM((NF * SLOTS + 16, PEERS), F32),
        ],
        "pack",
    )(owner, forcing)
    arrived = exchange(message, NF * SLOTS // 128, cols, 1)
    reply, soil_after = local_call(
        land_kernel,
        (shape((PEERS * 8, 128)), shape((LEVELS, ROWS))),
        [
            pltpu.VMEM((NF * SLOTS + 16, PEERS), BF16),
            pltpu.VMEM((PEERS, ROWS), BF16),
            pltpu.VMEM((SLOTS, ROWS), BF16),
            pltpu.VMEM((NF, LINES, 128), F32),
            pltpu.VMEM((NOUT, LINES, 128), F32),
            pltpu.VMEM((NOUT * SLOTS, WIDE), BF16),
            pltpu.VMEM((NF * SLOTS, PEERS), F32),
        ],
        "land",
    )(arrived, lines(sunlit), lines(plant_type), lines(leaf_area), soil_water, pft_table)
    returned = exchange(reply, 3, cols, 2)
    atm_flux = local_call(
        gather_kernel,
        shape((NOUT, ROWS // BROWS * BCOLS)),
        [pltpu.VMEM((384, PEERS), F32)],
        "gather",
    )(returned, owner, rank, lines(area), lines(column))
    return (atm_flux, soil_after)


def solution(mesh):
    spec = P(("row", "col"))
    wide = P(None, ("row", "col"))
    return jax.shard_map(
        functools.partial(body, mesh.shape["col"]),
        mesh=mesh,
        in_specs=(wide, spec, spec, spec, spec, spec, spec, wide, P()),
        out_specs=(wide, wide),
        check_vma=False,
    )
```

```python
import jax
import jax.numpy as jnp
from jax import lax
from jax.experimental import pallas as pl
from jax.experimental.pallas import tpu as pltpu
from jax.sharding import PartitionSpec as P

NF = 8
NOUT = 4
NPFT = 16
LEVELS = 15
ITERS = 4
SOILP = 4
BROWS = 512
BCOLS = 128
PEERS = 128
ROWS = 8192
LINES = ROWS // 128
SLOTS = 80
STEP = 256
WIDE = 1024
MESH = pl.DeviceIdType.MESH
F32 = jnp.float32
BF16 = jnp.bfloat16
NT = (((1,), (1,)), ((), ()))


def iota(shape, dim):
    return lax.broadcasted_iota(jnp.int32, shape, dim)


def as_bf16(mask):
    return jnp.where(mask, 1.0, 0.0).astype(BF16)


def dot(a, b):
    return jnp.dot(a, b, preferred_element_type=F32)


def dot_nt(a, b):
    return lax.dot_general(a, b, NT, preferred_element_type=F32)


def spread(hot, row):
    width = row.shape[1]
    tile = jnp.broadcast_to(row, (16, width)).astype(BF16)
    parts = hot.reshape(SLOTS // 16, 16, width) * tile[None]
    return parts.reshape(SLOTS, width)


def pack_kernel(owner_ref, forcing_ref, msg_ref, rank_ref, at_ref, w_ref, acc_ref):
    ids = iota((PEERS, 128), 0)
    for j in range(LINES):
        at_ref[:, 128 * j : 128 * j + 128] = as_bf16(ids == owner_ref[j : j + 1, :])
    base = jnp.zeros((PEERS, 128), F32)
    for g in range(ROWS // WIDE):
        earlier = as_bf16((iota((WIDE, 128), 0) + g * WIDE) // STEP < iota((WIDE, 128), 1))
        base = base + dot(at_ref[:, g * WIDE : (g + 1) * WIDE], earlier)
    upper = as_bf16(iota((STEP, STEP), 0) < iota((STEP, STEP), 1))
    slot = iota((SLOTS, STEP), 0).astype(F32)
    w_ref[NF * SLOTS :, :] = jnp.ones((16, WIDE), BF16)
    for g in range(ROWS // WIDE):
        for k in range(WIDE // STEP):
            c = g * (WIDE // STEP) + k
            a = at_ref[:, c * STEP : (c + 1) * STEP]
            seen = dot(a, upper) + base[:, c : c + 1]
            rank = jnp.sum(a.astype(F32) * seen, axis=0, keepdims=True)
            rank_ref[2 * c : 2 * c + 1, :] = rank[:, :128]
            rank_ref[2 * c + 1 : 2 * c + 2, :] = rank[:, 128:]
            hot = as_bf16(slot == rank)
            x = forcing_ref[:, c * STEP : (c + 1) * STEP].astype(F32)
            for f in range(NF):
                w_ref[f * SLOTS : (f + 1) * SLOTS, k * STEP : (k + 1) * STEP] = spread(hot, x[f : f + 1, :])
        part = dot_nt(w_ref[...], at_ref[:, g * WIDE : (g + 1) * WIDE])
        if g == 0:
            acc_ref[...] = part
        else:
            acc_ref[...] += part
    counts = acc_ref[NF * SLOTS : NF * SLOTS + 1, :]
    held = iota((SLOTS, PEERS), 0).astype(F32) < counts
    acc_ref[:SLOTS, :] = jnp.where(held, acc_ref[:SLOTS, :], -1.0)
    for i in range(NF * SLOTS // 128):
        msg_ref[pl.ds(i, PEERS, stride=8), :] = acc_ref[128 * i : 128 * (i + 1), :].T


def hops(step):
    return min(step, 4 - step)


OFFSETS = sorted(
    [(y, k, x, z) for y in range(4) for k in range(2) for x in range(4) for z in range(4)][1:],
    key=lambda o: -(3 * (hops(o[0]) + hops(o[2]) + hops(o[3])) + o[1]),
)


def place():
    row, col = lax.axis_index("row"), lax.axis_index("col")
    return row // 2, lax.rem(row, 2), col // 4, lax.rem(col, 4)


def neighbour(here, offset):
    y, k, x, z = (lax.rem(a + b, n) for a, b, n in zip(here, offset, (4, 2, 4, 4)))
    return y * 2 + k, x * 4 + z


def greet(here):
    barrier = pltpu.get_barrier_semaphore()
    for offset in OFFSETS:
        pl.semaphore_signal(barrier, inc=1, device_id=neighbour(here, offset), device_id_type=MESH)


def block(ref, index, lines):
    return ref.at[pl.ds(pl.multiple_of(index * 8, 8), lines), :]


def send_all(here, msg_ref, got_ref, lines, send_sem, recv_sem):
    row, col = neighbour(here, (0, 0, 0, 0))
    me = row * 16 + col
    for offset in OFFSETS:
        row, col = neighbour(here, offset)
        pltpu.make_async_remote_copy(
            src_ref=block(msg_ref, row * 16 + col, lines),
            dst_ref=block(got_ref, me, lines),
            send_sem=send_sem,
            recv_sem=recv_sem,
            device_id=(row, col),
            device_id_type=MESH,
        ).start()
    pltpu.make_async_copy(block(msg_ref, me, lines), block(got_ref, me, lines), recv_sem).start()


def await_all(msg_ref, got_ref, lines, send_sem, recv_sem):
    sent = msg_ref.at[: (PEERS - 1) * lines, :]
    pltpu.make_async_copy(sent, sent, send_sem).wait()
    got = got_ref.at[: PEERS * lines, :]
    pltpu.make_async_copy(got, got, recv_sem).wait()


def unfold(recv_ref, out_ref, lines):
    for i in range(lines):
        out_ref[128 * i : 128 * (i + 1), :] = recv_ref[pl.ds(i, PEERS, stride=8), :].T


def land_kernel(
    recv_ref, sunlit_ref, type_ref, leaf_ref, soil_ref, table_ref,
    msg_ref, after_ref,
    got_ref, p_ref, q_ref, field_ref, flux_ref, w_ref, acc_ref,
):
    unfold(recv_ref, acc_ref, NF * SLOTS // 128)
    counts = jnp.sum(jnp.where(acc_ref[:SLOTS, :] >= 0.0, 1.0, 0.0), axis=0, keepdims=True)
    below = iota((PEERS, PEERS), 1) < iota((PEERS, PEERS), 0)
    upto = iota((PEERS, PEERS), 1) <= iota((PEERS, PEERS), 0)
    after = as_bf16(iota((PEERS, PEERS), 0) < iota((PEERS, PEERS), 1))
    ones = jnp.ones((PEERS, STEP), BF16)
    begin = dot(jnp.where(below, counts, 0.0).astype(BF16), ones)
    end = dot(jnp.where(upto, counts, 0.0).astype(BF16), ones)
    begin_row = dot(jnp.broadcast_to(counts, (16, PEERS)).astype(BF16), after)
    high = jnp.floor(begin_row * (1.0 / 128.0))
    line = iota((16, PEERS), 0)
    tail = jnp.where(line == 0, high, jnp.where(line == 1, begin_row - 128.0 * high, 0.0))
    got_ref[: NF * SLOTS, :] = acc_ref[: NF * SLOTS, :].astype(BF16)
    got_ref[NF * SLOTS :, :] = tail.astype(BF16)
    slot = iota((SLOTS, STEP), 0).astype(F32)
    lane = iota((PEERS, STEP), 1).astype(F32)
    for c in range(ROWS // STEP):
        tile = lane + float(c * STEP)
        p = as_bf16((tile >= begin) & (tile < end))
        p_ref[:, c * STEP : (c + 1) * STEP] = p
        g = dot(got_ref[...], p)
        place = tile[:1, :] - (128.0 * g[NF * SLOTS : NF * SLOTS + 1, :] + g[NF * SLOTS + 1 : NF * SLOTS + 2, :])
        q = slot == place
        q_ref[:, c * STEP : (c + 1) * STEP] = as_bf16(q)
        for f in range(NF):
            value = jnp.sum(jnp.where(q, g[f * SLOTS : (f + 1) * SLOTS, :], 0.0), axis=0, keepdims=True)
            field_ref[f, 2 * c : 2 * c + 1, :] = value[:, :128]
            field_ref[f, 2 * c + 1 : 2 * c + 2, :] = value[:, 128:]

    table = jnp.concatenate([table_ref[...], jnp.zeros((4, 128 - NPFT), F32)], axis=1)
    single_t = jnp.sqrt(1.0 - (0.1 + 0.3 * table[0:1]))
    reflect_t = (1.0 - single_t) / (1.0 + single_t)
    vcmax_t = 0.5 + 1.5 * table[1:2]
    slope_t = 3.0 + 6.0 * table[2:3]
    kroot_t = 0.05 + 0.5 * table[3:4]
    level = iota((16, 128), 0)
    roots_t = jnp.where(level < LEVELS, jnp.exp(-kroot_t * level.astype(F32)), 0.0)
    roots_t = 0.05 * (roots_t / jnp.sum(roots_t, axis=0, keepdims=True))
    kinds = type_ref[...]

    def look(row):
        return jnp.take_along_axis(jnp.broadcast_to(row, (LINES, 128)), kinds, axis=1, mode="promise_in_bounds")

    single = look(single_t)
    reflect_h = look(reflect_t)
    vcmax = look(vcmax_t)
    slope = look(slope_t)
    leaf = leaf_ref[...]
    swdir = 2.0 * field_ref[0]
    swdif = field_ref[1]
    tair = field_ref[2] - 0.5
    vapour = 0.2 + field_ref[3]
    carbon = 0.8 + 0.4 * field_ref[4]
    coszen = 0.1 + 0.9 * field_ref[5]
    wind_speed = 0.5 + 2.0 * field_ref[6]
    extinct = 0.5 / coszen
    reflect_b = 2.0 * extinct * reflect_h / (1.0 + extinct)
    light = sunlit_ref[...].astype(F32) * (
        (1.0 - reflect_b) * swdir * (1.0 - jnp.exp(-extinct * single * leaf))
        + (1.0 - reflect_h) * swdif * (1.0 - jnp.exp(-0.8 * single * leaf))
    )
    electrons = 0.3 * light
    compensation = 0.08 * (1.0 + 0.3 * tair)
    capacity_t = vcmax * jnp.exp(0.5 * tair)
    internal = 0.7 * carbon
    for repeat in range(ITERS):
        limit = internal - compensation
        carboxyl = capacity_t * limit / (internal + 0.6)
        ribulose = electrons * limit / (4.0 * internal + 8.0 * compensation)
        assim = carboxyl * ribulose / (carboxyl + ribulose)
        conduct = 0.05 + slope * assim / carbon
        internal = carbon - 1.6 * assim / conduct
    transpire = conduct * vapour
    flux_ref[0] = assim
    flux_ref[1] = transpire
    flux_ref[2] = 0.5 * wind_speed * (0.2 * light - 0.5 * transpire)

    top = iota((16, 128), 0) == 0
    for j in range(LINES):
        kind = jnp.broadcast_to(type_ref[j : j + 1, :], (16, 128))
        draw = jnp.take_along_axis(roots_t, kind, axis=1, mode="promise_in_bounds")
        draw = (draw * flux_ref[1, j : j + 1, :])[:LEVELS]
        theta = soil_ref[:, 128 * j : 128 * (j + 1)]
        theta = theta + jnp.where(top, 0.1 * field_ref[7, j : j + 1, :], 0.0)[:LEVELS]
        for repeat in range(SOILP):
            above = jnp.concatenate([theta[:1], theta[:-1]], axis=0)
            under = jnp.concatenate([theta[1:], theta[-1:]], axis=0)
            theta = theta + 0.25 * (above + under - 2.0 * theta) - draw
        after_ref[:, 128 * j : 128 * (j + 1)] = theta
        flux_ref[3, j : j + 1, :] = 0.5 * theta[LEVELS - 1 :, :]

    for g in range(ROWS // WIDE):
        for k in range(WIDE // 128):
            j = g * (WIDE // 128) + k
            hot = q_ref[:, 128 * j : 128 * (j + 1)]
            for f in range(NOUT):
                w_ref[f * SLOTS : (f + 1) * SLOTS, 128 * k : 128 * (k + 1)] = spread(hot, flux_ref[f, j : j + 1, :])
        part = dot_nt(w_ref[: NOUT * SLOTS, :], p_ref[:, g * WIDE : (g + 1) * WIDE])
        if g == 0:
            acc_ref[: NOUT * SLOTS, :] = part
        else:
            acc_ref[: NOUT * SLOTS, :] += part
    for i in range(3):
        msg_ref[pl.ds(i, PEERS, stride=8), :] = acc_ref[128 * i : 128 * (i + 1), :].T


def gather_kernel(recv_ref, owner_ref, rank_ref, area_ref, column_ref, atm_ref, acc_ref):
    unfold(recv_ref, acc_ref, 3)
    got = acc_ref[: NOUT * SLOTS, :].astype(BF16)
    ids = iota((PEERS, 128), 0)
    slot = iota((SLOTS, 128), 0).astype(F32)
    for b in range(ROWS // BROWS):
        weights, targets = [], []
        for k in range(BROWS // STEP):
            c = b * (BROWS // STEP) + k
            a = jnp.concatenate(
                [as_bf16(ids == owner_ref[j : j + 1, :]) for j in (2 * c, 2 * c + 1)], axis=1
            )
            g = dot(got, a)
            q = jnp.concatenate([slot == rank_ref[j : j + 1, :] for j in (2 * c, 2 * c + 1)], axis=1)
            scale = jnp.concatenate([area_ref[j : j + 1, :] for j in (2 * c, 2 * c + 1)], axis=1)
            rows = [
                jnp.sum(jnp.where(q, g[f * SLOTS : (f + 1) * SLOTS, :], 0.0), axis=0, keepdims=True) * scale
                for f in range(NOUT)
            ]
            weights.append(jnp.concatenate(rows, axis=0))
            targets += [as_bf16(ids == column_ref[j : j + 1, :]) for j in (2 * c, 2 * c + 1)]
        weight = jnp.concatenate(weights, axis=1)
        high = weight.astype(BF16).astype(F32)
        both = jnp.concatenate([high, weight - high], axis=0).astype(BF16)
        total = dot_nt(both, jnp.concatenate(targets, axis=1))
        atm_ref[:, BCOLS * b : BCOLS * (b + 1)] = total[:NOUT] + total[NOUT:]


VMEM_LIMIT = 56 * 1024 * 1024


def step_kernel(
    owner_hbm, forcing_hbm, sunlit_hbm, type_hbm, leaf_hbm, soil_hbm, table_hbm, area_hbm, column_hbm,
    atm_ref, after_ref,
    owner_ref, forcing_ref, sunlit_ref, type_ref, leaf_ref, soil_ref, table_ref, area_ref, column_ref,
    in_sem, send_sem, recv_sem,
    msg_ref, got_ref, reply_ref, home_ref,
    rank_ref, at_ref, w_ref, acc_ref, lhs_ref, p_ref, q_ref, field_ref, flux_ref,
):
    copies = [
        pltpu.make_async_copy(a, b, in_sem.at[i])
        for i, (a, b) in enumerate(
            (
                (owner_hbm, owner_ref), (forcing_hbm, forcing_ref), (sunlit_hbm, sunlit_ref),
                (type_hbm, type_ref), (leaf_hbm, leaf_ref), (soil_hbm, soil_ref), (table_hbm, table_ref),
                (area_hbm, area_ref), (column_hbm, column_ref),
            )
        )
    ]
    for copy in copies:
        copy.start()
    here = place()
    greet(here)
    copies[0].wait()
    copies[1].wait()
    pack_kernel(owner_ref, forcing_ref, msg_ref, rank_ref, at_ref, w_ref, acc_ref)
    pl.semaphore_wait(pltpu.get_barrier_semaphore(), PEERS - 1)
    send_all(here, msg_ref, got_ref, 5, send_sem.at[0], recv_sem.at[0])
    for copy in copies[2:]:
        copy.wait()
    await_all(msg_ref, got_ref, 5, send_sem.at[0], recv_sem.at[0])
    land_kernel(
        got_ref, sunlit_ref, type_ref, leaf_ref, soil_ref, table_ref,
        reply_ref, after_ref,
        lhs_ref, p_ref, q_ref, field_ref, flux_ref, w_ref, acc_ref,
    )
    send_all(here, reply_ref, home_ref, 3, send_sem.at[1], recv_sem.at[1])
    await_all(reply_ref, home_ref, 3, send_sem.at[1], recv_sem.at[1])
    gather_kernel(home_ref, owner_ref, rank_ref, area_ref, column_ref, atm_ref, acc_ref)


def body(forcing, owner, column, area, sunlit, plant_type, leaf_area, soil_water, pft_table):
    lines = lambda x: x.reshape(LINES, 128)
    i32 = jnp.int32
    flat = lambda dtype: pltpu.VMEM((LINES, 128), dtype)
    message = pltpu.VMEM((PEERS * 8, 128), F32)
    return pl.pallas_call(
        step_kernel,
        out_shape=(
            jax.ShapeDtypeStruct((NOUT, ROWS // BROWS * BCOLS), F32),
            jax.ShapeDtypeStruct((LEVELS, ROWS), F32),
        ),
        in_specs=[pl.BlockSpec(memory_space=pl.ANY)] * 9,
        out_specs=(pl.BlockSpec(memory_space=pltpu.VMEM),) * 2,
        scratch_shapes=[
            flat(i32), pltpu.VMEM((NF, ROWS), BF16), flat(i32), flat(i32), flat(F32),
            pltpu.VMEM((LEVELS, ROWS), F32), pltpu.VMEM((4, NPFT), F32), flat(F32), flat(i32),
            pltpu.SemaphoreType.DMA((9,)), pltpu.SemaphoreType.DMA((2,)), pltpu.SemaphoreType.DMA((2,)),
            message, message, message, message,
            flat(F32),
            pltpu.VMEM((PEERS, ROWS), BF16),
            pltpu.VMEM((NF * SLOTS + 16, WIDE), BF16),
            pltpu.VMEM((NF * SLOTS + 16, PEERS), F32),
            pltpu.VMEM((NF * SLOTS + 16, PEERS), BF16),
            pltpu.VMEM((PEERS, ROWS), BF16),
            pltpu.VMEM((SLOTS, ROWS), BF16),
            pltpu.VMEM((NF, LINES, 128), F32),
            pltpu.VMEM((NOUT, LINES, 128), F32),
        ],
        compiler_params=pltpu.CompilerParams(
            collective_id=1, has_side_effects=True, vmem_limit_bytes=VMEM_LIMIT
        ),
        name="step",
    )(
        lines(owner), forcing, lines(sunlit), lines(plant_type), lines(leaf_area), soil_water, pft_table,
        lines(area), lines(column),
    )


def solution(mesh):
    spec = P(("row", "col"))
    wide = P(None, ("row", "col"))
    return jax.shard_map(
        body,
        mesh=mesh,
        in_specs=(wide, spec, spec, spec, spec, spec, spec, wide, P()),
        out_specs=(wide, wide),
        check_vma=False,
    )
```

```python
import jax
import jax.numpy as jnp
from jax import lax
from jax.experimental import pallas as pl
from jax.experimental.pallas import tpu as pltpu
from jax.sharding import PartitionSpec as P

NF = 8
NOUT = 4
NPFT = 16
LEVELS = 15
ITERS = 4
SOILP = 4
BROWS = 512
BCOLS = 128
PEERS = 128
ROWS = 8192
LINES = ROWS // 128
SLOTS = 80
QUADS = SLOTS // 4
STEP = 256
CHUNKS = ROWS // STEP
HALF = 2 * QUADS * NF
WINDOW = 64
SENT = NF * SLOTS // 128
BACK = 3
MESH = pl.DeviceIdType.MESH
F32 = jnp.float32
BF16 = jnp.bfloat16
NT = (((1,), (1,)), ((), ()))
VMEM_LIMIT = 56 * 1024 * 1024


def iota(shape, dim):
    return lax.broadcasted_iota(jnp.int32, shape, dim)


def as_bf16(mask):
    return jnp.where(mask, 1.0, 0.0).astype(BF16)


def dot(a, b):
    return jnp.dot(a, b, preferred_element_type=F32)


def dot_nt(a, b):
    return lax.dot_general(a, b, NT, preferred_element_type=F32)


def times_row(hot, row):
    rows, width = hot.shape
    tile = jnp.broadcast_to(row, (16, width)).astype(BF16)
    return (hot.reshape(rows // 16, 16, width) * tile[None]).reshape(rows, width)


def two_lines(ref, c):
    return jnp.concatenate([ref[2 * c : 2 * c + 1, :], ref[2 * c + 1 : 2 * c + 2, :]], axis=1)


def hops(step):
    return min(step, 4 - step)


OFFSETS = sorted(
    [(y, k, x, z) for y in range(4) for k in range(2) for x in range(4) for z in range(4)][1:],
    key=lambda o: -(3 * (hops(o[0]) + hops(o[2]) + hops(o[3])) + o[1]),
)


def place():
    row, col = lax.axis_index("row"), lax.axis_index("col")
    return row // 2, lax.rem(row, 2), col // 4, lax.rem(col, 4)


def neighbour(here, offset):
    y, k, x, z = (lax.rem(a + b, n) for a, b, n in zip(here, offset, (4, 2, 4, 4)))
    return y * 2 + k, x * 4 + z


def greet(here):
    barrier = pltpu.get_barrier_semaphore()
    for offset in OFFSETS:
        pl.semaphore_signal(barrier, inc=1, device_id=neighbour(here, offset), device_id_type=MESH)


def block(ref, index, lines):
    return ref.at[pl.ds(pl.multiple_of(index * 8, 8), lines), :]


def send_all(here, msg_ref, got_ref, lines, send_sem, recv_sem):
    row, col = neighbour(here, (0, 0, 0, 0))
    me = row * 16 + col
    for offset in OFFSETS:
        row, col = neighbour(here, offset)
        pltpu.make_async_remote_copy(
            src_ref=block(msg_ref, row * 16 + col, lines),
            dst_ref=block(got_ref, me, lines),
            send_sem=send_sem,
            recv_sem=recv_sem,
            device_id=(row, col),
            device_id_type=MESH,
        ).start()
    pltpu.make_async_copy(block(msg_ref, me, lines), block(got_ref, me, lines), recv_sem).start()


def await_all(msg_ref, got_ref, lines, send_sem, recv_sem):
    sent = msg_ref.at[: (PEERS - 1) * lines, :]
    pltpu.make_async_copy(sent, sent, send_sem).wait()
    got = got_ref.at[: PEERS * lines, :]
    pltpu.make_async_copy(got, got, recv_sem).wait()


def fold(values, msg_ref, lines):
    for i in range(lines):
        msg_ref[pl.ds(i, PEERS, stride=8), :] = values[128 * i : 128 * (i + 1), :].T


def unfold(got_ref, lines):
    return jnp.concatenate([got_ref[pl.ds(i, PEERS, stride=8), :].T for i in range(lines)], axis=0)


def pack(owner_ref, forcing_ref, msg_ref, pair_ref, a_ref, split_ref, w_ref):
    ids = iota((PEERS, 128), 0)
    for j in range(LINES):
        a_ref[:, 128 * j : 128 * (j + 1)] = as_bf16(ids == owner_ref[j : j + 1, :])
    upto = as_bf16(iota((STEP, STEP), 0) <= iota((STEP, STEP), 1))
    base = jnp.zeros((PEERS, 1), F32)
    for c in range(CHUNKS):
        a = a_ref[:, c * STEP : (c + 1) * STEP]
        seen = dot(a, upto)
        mine = (seen + base).astype(BF16) * a
        base = base + seen[:, STEP - 1 :]
        mine = mine.reshape(PEERS // 16, 16, STEP)
        total = mine[0]
        for i in range(1, PEERS // 16):
            total = total + mine[i]
        rank = jnp.sum(total.astype(F32), axis=0, keepdims=True) - 1.0
        pair = jnp.floor(rank * 0.5)
        odd = rank - 2.0 * pair
        pair_ref[2 * c : 2 * c + 1, :] = pair[:, :128]
        pair_ref[2 * c + 1 : 2 * c + 2, :] = pair[:, 128:]
        split_ref[:PEERS, c * STEP : (c + 1) * STEP] = times_row(a, 1.0 - odd)
        split_ref[PEERS:, c * STEP : (c + 1) * STEP] = times_row(a, odd)
    line = iota((16, STEP), 0)
    for c in range(CHUNKS):
        pair = jnp.broadcast_to(two_lines(pair_ref, c), (16, STEP)).astype(BF16)
        x = forcing_ref[:, c * STEP : (c + 1) * STEP].astype(F32)
        x = jnp.concatenate([x, x], axis=0).astype(BF16)
        for k in range(2 * QUADS // 2):
            label = 2 * (2 * (k % (QUADS // 2)) + line // 8) + k // (QUADS // 2)
            hit = label.astype(F32).astype(BF16) == pair
            w_ref[16 * k : 16 * (k + 1), c * STEP : (c + 1) * STEP] = jnp.where(hit, x, jnp.zeros((), BF16))
    w_ref[HALF:, :] = jnp.ones((16, ROWS), BF16)
    got = dot_nt(w_ref[...], split_ref[...])
    counts = got[HALF : HALF + 1, :PEERS] + got[HALF : HALF + 1, PEERS:]
    line = iota((HALF, PEERS), 0)
    label = 4 * (lax.rem(line, HALF // 2) // NF) + 2 * (line // (HALF // 2))
    values = [
        jnp.where((label + odd).astype(F32) < counts, got[:HALF, PEERS * odd : PEERS * (odd + 1)], -1.0)
        for odd in range(2)
    ]
    fold(jnp.concatenate(values, axis=0), msg_ref, SENT)


def look(row, kinds):
    return jnp.take_along_axis(jnp.broadcast_to(row, kinds.shape), kinds, axis=1, mode="promise_in_bounds")


def prepare(sunlit_ref, type_ref, leaf_ref, table_ref, early_ref, draw_ref):
    table = jnp.concatenate([table_ref[...], jnp.zeros((4, 128 - NPFT), F32)], axis=1)
    single_t = jnp.sqrt(1.0 - (0.1 + 0.3 * table[0:1]))
    reflect_t = (1.0 - single_t) / (1.0 + single_t)
    kroot_t = 0.05 + 0.5 * table[3:4]
    level = iota((16, 128), 0)
    roots_t = jnp.where(level < LEVELS, jnp.exp(-kroot_t * level.astype(F32)), 0.0)
    roots_t = 0.05 * (roots_t / jnp.sum(roots_t, axis=0, keepdims=True))
    kinds = type_ref[...]
    leaf = leaf_ref[...]
    single = look(single_t, kinds)
    reflect_h = look(reflect_t, kinds)
    lit = sunlit_ref[...].astype(F32)
    early_ref[0] = single * leaf
    early_ref[1] = reflect_h
    early_ref[2] = look(0.5 + 1.5 * table[1:2], kinds)
    early_ref[3] = look(3.0 + 6.0 * table[2:3], kinds)
    early_ref[4] = lit
    early_ref[5] = lit * (1.0 - reflect_h) * (1.0 - jnp.exp(-0.8 * single * leaf))
    for j in range(LINES):
        draw_ref[:, 128 * j : 128 * (j + 1)] = look(roots_t, jnp.broadcast_to(type_ref[j : j + 1, :], (16, 128)))


def window_of(c):
    least = c * STEP // SLOTS
    most = min(PEERS - 1, (PEERS * SLOTS - ROWS + c * STEP + STEP - 1) // SLOTS)
    for w in range(3):
        if 32 * w <= least and most < 32 * w + WINDOW:
            return w
    raise ValueError


def arrange(got_ref, lhs_ref):
    got = unfold(got_ref, SENT)
    valid = jnp.where(got >= 0.0, 1.0 / NF, 0.0)
    counts = jnp.sum(valid, axis=0, keepdims=True)
    part = lambda odd, a: got[HALF * odd + HALF // 2 * a : HALF * odd + HALF // 2 * (a + 1), :]
    low = iota((HALF // 2, 128), 1) < WINDOW
    for a in range(2):
        even, odd = part(0, a), part(1, a)
        for w in range(3):
            left = even if w == 0 else pltpu.roll(even, 128 - 32 * w, 1)
            right = odd if w == 2 else pltpu.roll(odd, 64 - 32 * w, 1)
            lhs_ref[w, :, 128 * a : 128 * (a + 1)] = jnp.where(low, left, right).astype(BF16)
    before = iota((PEERS, PEERS), 1) < iota((PEERS, PEERS), 0)
    upto = iota((PEERS, PEERS), 1) <= iota((PEERS, PEERS), 0)
    ones = jnp.ones((PEERS, STEP), BF16)
    begin = dot(jnp.where(before, counts, 0.0).astype(BF16), ones)
    end = dot(jnp.where(upto, counts, 0.0).astype(BF16), ones)
    return begin, end


def unpack(got_ref, lhs_ref, p_ref, quad_ref, field_ref):
    begin, end = arrange(got_ref, lhs_ref)
    for c in range(CHUNKS):
        w = window_of(c)
        first = begin[32 * w : 32 * w + WINDOW]
        tile = (iota((1, STEP), 1) + c * STEP).astype(F32)
        mine = (tile >= first) & (tile < end[32 * w : 32 * w + WINDOW])
        slot = tile - jnp.sum(jnp.where(mine, first, 0.0), axis=0, keepdims=True)
        quad = jnp.floor(slot * 0.25)
        rest = slot - 4.0 * quad
        quad_ref[2 * c : 2 * c + 1, :] = quad[:, :128]
        quad_ref[2 * c + 1 : 2 * c + 2, :] = quad[:, 128:]
        hot = as_bf16(mine)
        for k in range(4):
            p_ref[WINDOW * k : WINDOW * (k + 1), c * STEP : (c + 1) * STEP] = times_row(
                hot, jnp.where(rest == float(k), 1.0, 0.0)
            )
    for c in range(CHUNKS):
        g = dot(lhs_ref[window_of(c)], p_ref[:, c * STEP : (c + 1) * STEP])
        quad = jnp.broadcast_to(two_lines(quad_ref, c), (NF, STEP))
        value = jnp.zeros((NF, STEP), F32)
        for s in range(QUADS):
            value = value + jnp.where(quad == float(s), g[NF * s : NF * (s + 1), :], 0.0)
        field_ref[NF * 2 * c : NF * (2 * c + 1), :] = value[:, :128]
        field_ref[NF * (2 * c + 1) : NF * (2 * c + 2), :] = value[:, 128:]


def physics(early_ref, field_ref, flux_ref):
    field = lambda f: field_ref[pl.ds(f, LINES, stride=NF), :]
    thick, reflect_h, vcmax, slope, lit, diffuse = (early_ref[i] for i in range(6))
    swdir = 2.0 * field(0)
    tair = field(2) - 0.5
    vapour = 0.2 + field(3)
    carbon = 0.8 + 0.4 * field(4)
    coszen = 0.1 + 0.9 * field(5)
    wind_speed = 0.5 + 2.0 * field(6)
    extinct = 0.5 / coszen
    reflect_b = 2.0 * extinct * reflect_h / (1.0 + extinct)
    light = lit * (1.0 - reflect_b) * swdir * (1.0 - jnp.exp(-extinct * thick)) + diffuse * field(1)
    electrons = 0.3 * light
    compensation = 0.08 * (1.0 + 0.3 * tair)
    capacity_t = vcmax * jnp.exp(0.5 * tair)
    internal = 0.7 * carbon
    for repeat in range(ITERS):
        limit = internal - compensation
        carboxyl = capacity_t * limit / (internal + 0.6)
        ribulose = electrons * limit / (4.0 * internal + 8.0 * compensation)
        assim = carboxyl * ribulose / (carboxyl + ribulose)
        conduct = 0.05 + slope * assim / carbon
        internal = carbon - 1.6 * assim / conduct
    transpire = conduct * vapour
    for f, value in enumerate((assim, transpire, 0.5 * wind_speed * (0.2 * light - 0.5 * transpire))):
        flux_ref[pl.ds(f, LINES, stride=8), :] = value
        flux_ref[pl.ds(f + NOUT, LINES, stride=8), :] = value


def soil_pass(theta, draw, level):
    above = jnp.where(level == 0, theta, pltpu.roll(theta, 1, 0))
    under = jnp.where(level == LEVELS - 1, theta, pltpu.roll(theta, theta.shape[0] - 1, 0))
    return theta + 0.25 * (above + under - 2.0 * theta) - draw


def drain(soil_ref, draw_ref, flux_ref):
    level = iota((8, 128), 0) + 8
    for j in range(LINES):
        lanes = slice(128 * j, 128 * (j + 1))
        draw = draw_ref[8:, lanes] * flux_ref[8 * j + 1 : 8 * j + 2, :]
        theta = jnp.concatenate([soil_ref[8:, lanes], jnp.zeros((1, 128), F32)], axis=0)
        for repeat in range(SOILP):
            theta = soil_pass(theta, draw, level)
        value = 0.5 * theta[LEVELS - 9 : LEVELS - 8, :]
        flux_ref[8 * j + 3 : 8 * j + 4, :] = value
        flux_ref[8 * j + 7 : 8 * j + 8, :] = value


def soil(soil_ref, draw_ref, field_ref, flux_ref):
    level = iota((16, 128), 0)
    for j in range(LINES):
        lanes = slice(128 * j, 128 * (j + 1))
        draw = draw_ref[:, lanes] * flux_ref[8 * j + 1 : 8 * j + 2, :]
        theta = jnp.concatenate([soil_ref[:, lanes], jnp.zeros((1, 128), F32)], axis=0)
        theta = theta + jnp.where(level == 0, 0.1 * field_ref[NF * j + 7 : NF * j + 8, :], 0.0)
        for repeat in range(SOILP):
            theta = soil_pass(theta, draw, level)
        soil_ref[:, lanes] = theta[:LEVELS]


def reply(flux_ref, quad_ref, p_ref, w_ref, msg_ref):
    line = iota((8, 128), 0)
    for j in range(LINES):
        flux = flux_ref[8 * j : 8 * (j + 1), :]
        quad = jnp.broadcast_to(quad_ref[j : j + 1, :], (8, 128))
        parts = [
            jnp.where((2 * k + line // NOUT).astype(F32) == quad, flux, 0.0) for k in range(QUADS // 2)
        ]
        w_ref[: NOUT * QUADS, 128 * j : 128 * (j + 1)] = jnp.concatenate(parts, axis=0).astype(BF16)
    low = iota((NOUT * QUADS, 128), 1)
    total = [[], [], [], []]
    for w in range(3):
        mine = [c for c in range(CHUNKS) if window_of(c) == w]
        lanes = slice(mine[0] * STEP, (mine[-1] + 1) * STEP)
        g = dot_nt(w_ref[: NOUT * QUADS, lanes], p_ref[:, lanes])
        for k in range(4):
            half = g[:, 128 * (k // 2) : 128 * (k // 2 + 1)]
            start = WINDOW * (k % 2)
            half = jnp.where((low >= start) & (low < start + WINDOW), half, 0.0)
            shift = (32 * w - start) % 128
            total[k].append(pltpu.roll(half, shift, 1) if shift else half)
    values = [a + b + c for a, b, c in total]
    values.append(jnp.zeros((BACK * 128 - NOUT * SLOTS, PEERS), F32))
    fold(jnp.concatenate(values, axis=0), msg_ref, BACK)


def targets(column_ref, target_ref):
    ids = iota((BCOLS, 128), 0)
    for j in range(LINES):
        target_ref[:, 128 * j : 128 * (j + 1)] = as_bf16(ids == column_ref[j : j + 1, :])


def gather(home_ref, pair_ref, area_ref, split_ref, target_ref, atm_ref):
    got = unfold(home_ref, BACK)
    rows = NOUT * QUADS
    part = lambda k: got[rows * k : rows * (k + 1), :]
    even = jnp.concatenate([part(0), part(2)], axis=0)
    odd = jnp.concatenate([part(1), part(3)], axis=0)
    lhs = jnp.concatenate([even, odd], axis=1).astype(BF16)
    line = iota((8, STEP), 0)
    for b in range(ROWS // BROWS):
        both = []
        for c in (2 * b, 2 * b + 1):
            g = dot(lhs, split_ref[:, c * STEP : (c + 1) * STEP])
            pair = jnp.broadcast_to(two_lines(pair_ref, c), (8, STEP))
            value = jnp.zeros((8, STEP), F32)
            for k in range(QUADS):
                label = 2 * (2 * (k % (QUADS // 2)) + line // NOUT) + k // (QUADS // 2)
                value = value + jnp.where(label.astype(F32) == pair, g[8 * k : 8 * (k + 1), :], 0.0)
            value = (value + pltpu.roll(value, NOUT, 0)) * two_lines(area_ref, c)
            high = value.astype(BF16).astype(F32)
            both.append(jnp.where(line < NOUT, high, value - high).astype(BF16))
        total = dot_nt(jnp.concatenate(both, axis=1), target_ref[:, b * BROWS : (b + 1) * BROWS])
        atm_ref[:, BCOLS * b : BCOLS * (b + 1)] = total[:NOUT] + total[NOUT:]


def step_kernel(
    owner_hbm, forcing_hbm, sunlit_hbm, type_hbm, leaf_hbm, soil_hbm, table_hbm, area_hbm, column_hbm,
    atm_ref, after_hbm,
    owner_ref, forcing_ref, sunlit_ref, type_ref, leaf_ref, soil_ref, table_ref, area_ref, column_ref,
    in_sem, out_sem, send_sem, recv_sem,
    msg_ref, got_ref, reply_ref, home_ref,
    pair_ref, quad_ref, a_ref, split_ref, w_ref, lhs_ref, p_ref, early_ref, draw_ref, field_ref, flux_ref,
):
    copies = [
        pltpu.make_async_copy(a, b, in_sem.at[i])
        for i, (a, b) in enumerate(
            (
                (owner_hbm, owner_ref), (forcing_hbm, forcing_ref), (sunlit_hbm, sunlit_ref),
                (type_hbm, type_ref), (leaf_hbm, leaf_ref), (soil_hbm, soil_ref),
                (table_hbm, table_ref), (area_hbm, area_ref), (column_hbm, column_ref),
            )
        )
    ]
    for copy in copies:
        copy.start()
    here = place()
    greet(here)
    copies[0].wait()
    copies[1].wait()
    pack(owner_ref, forcing_ref, msg_ref, pair_ref, a_ref, split_ref, w_ref)
    pl.semaphore_wait(pltpu.get_barrier_semaphore(), PEERS - 1)
    send_all(here, msg_ref, got_ref, SENT, send_sem.at[0], recv_sem.at[0])
    for copy in copies[2:]:
        copy.wait()
    prepare(sunlit_ref, type_ref, leaf_ref, table_ref, early_ref, draw_ref)
    await_all(msg_ref, got_ref, SENT, send_sem.at[0], recv_sem.at[0])
    unpack(got_ref, lhs_ref, p_ref, quad_ref, field_ref)
    physics(early_ref, field_ref, flux_ref)
    drain(soil_ref, draw_ref, flux_ref)
    reply(flux_ref, quad_ref, p_ref, w_ref, reply_ref)
    send_all(here, reply_ref, home_ref, BACK, send_sem.at[1], recv_sem.at[1])
    soil(soil_ref, draw_ref, field_ref, flux_ref)
    after = pltpu.make_async_copy(soil_ref, after_hbm, out_sem)
    after.start()
    targets(column_ref, a_ref)
    await_all(reply_ref, home_ref, BACK, send_sem.at[1], recv_sem.at[1])
    gather(home_ref, pair_ref, area_ref, split_ref, a_ref, atm_ref)
    after.wait()


def body(forcing, owner, column, area, sunlit, plant_type, leaf_area, soil_water, pft_table):
    lines = lambda x: x.reshape(LINES, 128)
    i32 = jnp.int32
    flat = lambda dtype: pltpu.VMEM((LINES, 128), dtype)
    message = pltpu.VMEM((PEERS * 8, 128), F32)
    sem = pltpu.SemaphoreType.DMA
    return pl.pallas_call(
        step_kernel,
        out_shape=(
            jax.ShapeDtypeStruct((NOUT, ROWS // BROWS * BCOLS), F32),
            jax.ShapeDtypeStruct((LEVELS, ROWS), F32),
        ),
        in_specs=[pl.BlockSpec(memory_space=pl.ANY)] * 9,
        out_specs=(pl.BlockSpec(memory_space=pltpu.VMEM), pl.BlockSpec(memory_space=pl.ANY)),
        scratch_shapes=[
            flat(i32), pltpu.VMEM((NF, ROWS), BF16), flat(i32), flat(i32), flat(F32),
            pltpu.VMEM((LEVELS, ROWS), F32), pltpu.VMEM((4, NPFT), F32), flat(F32), flat(i32),
            sem((9,)), sem, sem((2,)), sem((2,)),
            message, message, message, message,
            flat(F32), flat(F32),
            pltpu.VMEM((PEERS, ROWS), BF16),
            pltpu.VMEM((2 * PEERS, ROWS), BF16),
            pltpu.VMEM((HALF + 16, ROWS), BF16),
            pltpu.VMEM((3, HALF // 2, STEP), BF16),
            pltpu.VMEM((4 * WINDOW, ROWS), BF16),
            pltpu.VMEM((6, LINES, 128), F32),
            pltpu.VMEM((16, ROWS), F32),
            pltpu.VMEM((LINES * NF, 128), F32),
            pltpu.VMEM((LINES * 8, 128), F32),
        ],
        compiler_params=pltpu.CompilerParams(
            collective_id=1, has_side_effects=True, vmem_limit_bytes=VMEM_LIMIT
        ),
        name="step",
    )(
        lines(owner), forcing, lines(sunlit), lines(plant_type), lines(leaf_area), soil_water, pft_table,
        lines(area), lines(column),
    )


def solution(mesh):
    spec = P(("row", "col"))
    wide = P(None, ("row", "col"))
    return jax.shard_map(
        body,
        mesh=mesh,
        in_specs=(wide, spec, spec, spec, spec, spec, spec, wide, P()),
        out_specs=(wide, wide),
        check_vma=False,
    )
```

```python
import jax
import jax.numpy as jnp
from jax import lax
from jax.experimental import pallas as pl
from jax.experimental.pallas import tpu as pltpu
from jax.sharding import PartitionSpec as P

NF = 8
NOUT = 4
NPFT = 16
LEVELS = 15
ITERS = 4
SOILP = 4
BROWS = 512
BCOLS = 128
PEERS = 128
ROWS = 8192
LINES = ROWS // 128
SLOTS = 80
QUADS = SLOTS // 4
STEP = 256
CHUNKS = ROWS // STEP
HALF = 2 * QUADS * NF
WINDOW = 64
SENT = NF * SLOTS // 128
BACK = 3
PARTS = 4
MESH = pl.DeviceIdType.MESH
F32 = jnp.float32
BF16 = jnp.bfloat16
NT = (((1,), (1,)), ((), ()))
VMEM_LIMIT = 56 * 1024 * 1024


def iota(shape, dim):
    return lax.broadcasted_iota(jnp.int32, shape, dim)


def as_bf16(mask):
    return jnp.where(mask, 1.0, 0.0).astype(BF16)


def dot(a, b):
    return jnp.dot(a, b, preferred_element_type=F32)


def dot_nt(a, b):
    return lax.dot_general(a, b, NT, preferred_element_type=F32)


def times_row(hot, row):
    rows, width = hot.shape
    tile = jnp.broadcast_to(row, (16, width)).astype(BF16)
    return (hot.reshape(rows // 16, 16, width) * tile[None]).reshape(rows, width)


def two_lines(ref, c):
    return jnp.concatenate([ref[2 * c : 2 * c + 1, :], ref[2 * c + 1 : 2 * c + 2, :]], axis=1)


def hops(step):
    return min(step, 4 - step)


OFFSETS = sorted(
    [(y, k, x, z) for y in range(4) for k in range(2) for x in range(4) for z in range(4)][1:],
    key=lambda o: -(3 * (hops(o[0]) + hops(o[2]) + hops(o[3])) + o[1]),
)


def place():
    row, col = lax.axis_index("row"), lax.axis_index("col")
    return row // 2, lax.rem(row, 2), col // 4, lax.rem(col, 4)


def neighbour(here, offset):
    y, k, x, z = (lax.rem(a + b, n) for a, b, n in zip(here, offset, (4, 2, 4, 4)))
    return y * 2 + k, x * 4 + z


def greet(here):
    barrier = pltpu.get_barrier_semaphore()
    for offset in OFFSETS:
        pl.semaphore_signal(barrier, inc=1, device_id=neighbour(here, offset), device_id_type=MESH)


def block(ref, index, lines):
    return ref.at[pl.ds(pl.multiple_of(index * 8, 8), lines), :]


def send_all(here, msg_ref, got_ref, lines, send_sem, recv_sem):
    row, col = neighbour(here, (0, 0, 0, 0))
    me = row * 16 + col
    for offset in OFFSETS:
        row, col = neighbour(here, offset)
        pltpu.make_async_remote_copy(
            src_ref=block(msg_ref, row * 16 + col, lines),
            dst_ref=block(got_ref, me, lines),
            send_sem=send_sem,
            recv_sem=recv_sem,
            device_id=(row, col),
            device_id_type=MESH,
        ).start()
    pltpu.make_async_copy(block(msg_ref, me, lines), block(got_ref, me, lines), recv_sem).start()


def await_all(msg_ref, got_ref, lines, send_sem, recv_sem):
    sent = msg_ref.at[: (PEERS - 1) * lines, :]
    pltpu.make_async_copy(sent, sent, send_sem).wait()
    got = got_ref.at[: PEERS * lines, :]
    pltpu.make_async_copy(got, got, recv_sem).wait()


def fold(values, msg_ref, lines):
    for i in range(lines):
        msg_ref[pl.ds(i, PEERS, stride=8), :] = values[128 * i : 128 * (i + 1), :].T


def unfold(got_ref, lines):
    return jnp.concatenate([got_ref[pl.ds(i, PEERS, stride=8), :].T for i in range(lines)], axis=0)


def pack(owner_ref, forcing_ref, msg_ref, pair_ref, a_ref, split_ref, w_ref):
    ids = iota((PEERS, 128), 0)
    for j in range(LINES):
        a_ref[:, 128 * j : 128 * (j + 1)] = as_bf16(ids == owner_ref[j : j + 1, :])
    upto = as_bf16(iota((STEP, STEP), 0) <= iota((STEP, STEP), 1))
    base = jnp.zeros((PEERS, 1), F32)
    for c in range(CHUNKS):
        a = a_ref[:, c * STEP : (c + 1) * STEP]
        seen = dot(a, upto)
        mine = (seen + base).astype(BF16) * a
        base = base + seen[:, STEP - 1 :]
        mine = mine.reshape(PEERS // 16, 16, STEP)
        total = mine[0]
        for i in range(1, PEERS // 16):
            total = total + mine[i]
        rank = jnp.sum(total.astype(F32), axis=0, keepdims=True) - 1.0
        pair = jnp.floor(rank * 0.5)
        odd = rank - 2.0 * pair
        pair_ref[2 * c : 2 * c + 1, :] = pair[:, :128]
        pair_ref[2 * c + 1 : 2 * c + 2, :] = pair[:, 128:]
        split_ref[:PEERS, c * STEP : (c + 1) * STEP] = times_row(a, 1.0 - odd)
        split_ref[PEERS:, c * STEP : (c + 1) * STEP] = times_row(a, odd)
    line = iota((16, STEP), 0)
    for c in range(CHUNKS):
        pair = jnp.broadcast_to(two_lines(pair_ref, c), (16, STEP)).astype(BF16)
        x = forcing_ref[:, c * STEP : (c + 1) * STEP].astype(F32)
        x = jnp.concatenate([x, x], axis=0).astype(BF16)
        for k in range(2 * QUADS // 2):
            label = 2 * (2 * (k % (QUADS // 2)) + line // 8) + k // (QUADS // 2)
            hit = label.astype(F32).astype(BF16) == pair
            w_ref[16 * k : 16 * (k + 1), c * STEP : (c + 1) * STEP] = jnp.where(hit, x, jnp.zeros((), BF16))
    w_ref[HALF:, :] = jnp.ones((16, ROWS), BF16)
    got = dot_nt(w_ref[...], split_ref[...])
    counts = got[HALF : HALF + 1, :PEERS] + got[HALF : HALF + 1, PEERS:]
    line = iota((HALF, PEERS), 0)
    label = 4 * (lax.rem(line, HALF // 2) // NF) + 2 * (line // (HALF // 2))
    values = [
        jnp.where((label + odd).astype(F32) < counts, got[:HALF, PEERS * odd : PEERS * (odd + 1)], -1.0)
        for odd in range(2)
    ]
    fold(jnp.concatenate(values, axis=0), msg_ref, SENT)


def look(row, kinds):
    return jnp.take_along_axis(jnp.broadcast_to(row, kinds.shape), kinds, axis=1, mode="promise_in_bounds")


def prepare(sunlit_ref, type_ref, leaf_ref, table_ref, early_ref, draw_ref):
    table = jnp.concatenate([table_ref[...], jnp.zeros((4, 128 - NPFT), F32)], axis=1)
    single_t = jnp.sqrt(1.0 - (0.1 + 0.3 * table[0:1]))
    reflect_t = (1.0 - single_t) / (1.0 + single_t)
    kroot_t = 0.05 + 0.5 * table[3:4]
    level = iota((16, 128), 0)
    roots_t = jnp.where(level < LEVELS, jnp.exp(-kroot_t * level.astype(F32)), 0.0)
    roots_t = 0.05 * (roots_t / jnp.sum(roots_t, axis=0, keepdims=True))
    kinds = type_ref[...]
    leaf = leaf_ref[...]
    single = look(single_t, kinds)
    reflect_h = look(reflect_t, kinds)
    lit = sunlit_ref[...].astype(F32)
    early_ref[0] = single * leaf
    early_ref[1] = reflect_h
    early_ref[2] = look(0.5 + 1.5 * table[1:2], kinds)
    early_ref[3] = look(3.0 + 6.0 * table[2:3], kinds)
    early_ref[4] = lit
    early_ref[5] = lit * (1.0 - reflect_h) * (1.0 - jnp.exp(-0.8 * single * leaf))
    for j in range(LINES):
        draw_ref[:, 128 * j : 128 * (j + 1)] = look(roots_t, jnp.broadcast_to(type_ref[j : j + 1, :], (16, 128)))


def window_of(c):
    least = c * STEP // SLOTS
    most = min(PEERS - 1, (PEERS * SLOTS - ROWS + c * STEP + STEP - 1) // SLOTS)
    for w in range(3):
        if 32 * w <= least and most < 32 * w + WINDOW:
            return w
    raise ValueError


def arrange(got_ref, lhs_ref):
    got = unfold(got_ref, SENT)
    valid = jnp.where(got >= 0.0, 1.0 / NF, 0.0)
    counts = jnp.sum(valid, axis=0, keepdims=True)
    part = lambda odd, a: got[HALF * odd + HALF // 2 * a : HALF * odd + HALF // 2 * (a + 1), :]
    low = iota((HALF // 2, 128), 1) < WINDOW
    for a in range(2):
        even, odd = part(0, a), part(1, a)
        for w in range(3):
            left = even if w == 0 else pltpu.roll(even, 128 - 32 * w, 1)
            right = odd if w == 2 else pltpu.roll(odd, 64 - 32 * w, 1)
            lhs_ref[w, :, 128 * a : 128 * (a + 1)] = jnp.where(low, left, right).astype(BF16)
    before = iota((PEERS, PEERS), 1) < iota((PEERS, PEERS), 0)
    upto = iota((PEERS, PEERS), 1) <= iota((PEERS, PEERS), 0)
    ones = jnp.ones((PEERS, STEP), BF16)
    begin = dot(jnp.where(before, counts, 0.0).astype(BF16), ones)
    end = dot(jnp.where(upto, counts, 0.0).astype(BF16), ones)
    return begin, end


def unpack(got_ref, lhs_ref, p_ref, quad_ref, field_ref):
    begin, end = arrange(got_ref, lhs_ref)
    for c in range(CHUNKS):
        w = window_of(c)
        first = begin[32 * w : 32 * w + WINDOW]
        tile = (iota((1, STEP), 1) + c * STEP).astype(F32)
        mine = (tile >= first) & (tile < end[32 * w : 32 * w + WINDOW])
        slot = tile - jnp.sum(jnp.where(mine, first, 0.0), axis=0, keepdims=True)
        quad = jnp.floor(slot * 0.25)
        rest = slot - 4.0 * quad
        quad_ref[2 * c : 2 * c + 1, :] = quad[:, :128]
        quad_ref[2 * c + 1 : 2 * c + 2, :] = quad[:, 128:]
        hot = as_bf16(mine)
        for k in range(4):
            p_ref[WINDOW * k : WINDOW * (k + 1), c * STEP : (c + 1) * STEP] = times_row(
                hot, jnp.where(rest == float(k), 1.0, 0.0)
            )
    for c in range(CHUNKS):
        g = dot(lhs_ref[window_of(c)], p_ref[:, c * STEP : (c + 1) * STEP])
        quad = jnp.broadcast_to(two_lines(quad_ref, c), (NF, STEP))
        value = jnp.zeros((NF, STEP), F32)
        for s in range(QUADS):
            value = value + jnp.where(quad == float(s), g[NF * s : NF * (s + 1), :], 0.0)
        field_ref[NF * 2 * c : NF * (2 * c + 1), :] = value[:, :128]
        field_ref[NF * (2 * c + 1) : NF * (2 * c + 2), :] = value[:, 128:]


def physics(early_ref, field_ref, flux_ref):
    field = lambda f: field_ref[pl.ds(f, LINES, stride=NF), :]
    thick, reflect_h, vcmax, slope, lit, diffuse = (early_ref[i] for i in range(6))
    swdir = 2.0 * field(0)
    tair = field(2) - 0.5
    vapour = 0.2 + field(3)
    carbon = 0.8 + 0.4 * field(4)
    coszen = 0.1 + 0.9 * field(5)
    wind_speed = 0.5 + 2.0 * field(6)
    extinct = 0.5 / coszen
    reflect_b = 2.0 * extinct * reflect_h / (1.0 + extinct)
    light = lit * (1.0 - reflect_b) * swdir * (1.0 - jnp.exp(-extinct * thick)) + diffuse * field(1)
    electrons = 0.3 * light
    compensation = 0.08 * (1.0 + 0.3 * tair)
    capacity_t = vcmax * jnp.exp(0.5 * tair)
    internal = 0.7 * carbon
    for repeat in range(ITERS):
        limit = internal - compensation
        carboxyl = capacity_t * limit / (internal + 0.6)
        ribulose = electrons * limit / (4.0 * internal + 8.0 * compensation)
        assim = carboxyl * ribulose / (carboxyl + ribulose)
        conduct = 0.05 + slope * assim / carbon
        internal = carbon - 1.6 * assim / conduct
    transpire = conduct * vapour
    for f, value in enumerate((assim, transpire, 0.5 * wind_speed * (0.2 * light - 0.5 * transpire))):
        flux_ref[pl.ds(f, LINES, stride=8), :] = value
        flux_ref[pl.ds(f + NOUT, LINES, stride=8), :] = value


def soil_pass(theta, draw, level):
    above = jnp.where(level == 0, theta, pltpu.roll(theta, 1, 0))
    under = jnp.where(level == LEVELS - 1, theta, pltpu.roll(theta, theta.shape[0] - 1, 0))
    return theta + 0.25 * (above + under - 2.0 * theta) - draw


def drain(soil_ref, draw_ref, flux_ref):
    level = iota((8, 128), 0) + 8
    for j in range(LINES):
        lanes = slice(128 * j, 128 * (j + 1))
        draw = draw_ref[8:, lanes] * flux_ref[8 * j + 1 : 8 * j + 2, :]
        theta = jnp.concatenate([soil_ref[8:, lanes], jnp.zeros((1, 128), F32)], axis=0)
        for repeat in range(SOILP):
            theta = soil_pass(theta, draw, level)
        value = 0.5 * theta[LEVELS - 9 : LEVELS - 8, :]
        flux_ref[8 * j + 3 : 8 * j + 4, :] = value
        flux_ref[8 * j + 7 : 8 * j + 8, :] = value


def soil(soil_ref, draw_ref, field_ref, flux_ref):
    level = iota((16, 128), 0)
    for j in range(LINES):
        lanes = slice(128 * j, 128 * (j + 1))
        draw = draw_ref[:, lanes] * flux_ref[8 * j + 1 : 8 * j + 2, :]
        theta = jnp.concatenate([soil_ref[:, lanes], jnp.zeros((1, 128), F32)], axis=0)
        theta = theta + jnp.where(level == 0, 0.1 * field_ref[NF * j + 7 : NF * j + 8, :], 0.0)
        for repeat in range(SOILP):
            theta = soil_pass(theta, draw, level)
        soil_ref[:, lanes] = theta[:LEVELS]


def reply(flux_ref, quad_ref, p_ref, w_ref, msg_ref):
    line = iota((8, 128), 0)
    for j in range(LINES):
        flux = flux_ref[8 * j : 8 * (j + 1), :]
        quad = jnp.broadcast_to(quad_ref[j : j + 1, :], (8, 128))
        parts = [
            jnp.where((2 * k + line // NOUT).astype(F32) == quad, flux, 0.0) for k in range(QUADS // 2)
        ]
        w_ref[: NOUT * QUADS, 128 * j : 128 * (j + 1)] = jnp.concatenate(parts, axis=0).astype(BF16)
    held = []
    for w in range(3):
        mine = [c for c in range(CHUNKS) if window_of(c) == w]
        lanes = slice(mine[0] * STEP, (mine[-1] + 1) * STEP)
        held.append(dot_nt(p_ref[:, lanes], w_ref[: NOUT * QUADS, lanes]))
    parts = []
    for k in range(4):
        a, b, c = (g[WINDOW * k : WINDOW * (k + 1)] for g in held)
        rows = jnp.concatenate([a[:32], a[32:] + b[:32], b[32:] + c[:32], c[32:]], axis=0)
        rows = jnp.concatenate([rows, jnp.zeros((PEERS, 128 - NOUT * QUADS), F32)], axis=1)
        shift = NOUT * QUADS * k % 128
        parts.append(pltpu.roll(rows, shift, 1) if shift else rows)
    lane = iota((PEERS, 128), 1)
    lines = (
        jnp.where(lane < 80, parts[0], parts[1]),
        jnp.where(lane < 32, parts[1], jnp.where(lane < 112, parts[2], parts[3])),
        parts[3],
    )
    for i in range(BACK):
        msg_ref[pl.ds(i, PEERS, stride=8), :] = lines[i]


def targets(column_ref, target_ref):
    ids = iota((BCOLS, 128), 0)
    for j in range(LINES):
        target_ref[:, 128 * j : 128 * (j + 1)] = as_bf16(ids == column_ref[j : j + 1, :])


def gather(home_ref, pair_ref, area_ref, split_ref, target_ref, atm_ref, both_ref):
    got = unfold(home_ref, BACK)
    rows = NOUT * QUADS
    part = lambda k: got[rows * k : rows * (k + 1), :]
    even = jnp.concatenate([part(0), part(2)], axis=0)
    odd = jnp.concatenate([part(1), part(3)], axis=0)
    lhs = jnp.concatenate([even, odd], axis=1).astype(BF16)
    line = iota((8, STEP), 0)
    for c in range(CHUNKS):
        g = dot(lhs, split_ref[:, c * STEP : (c + 1) * STEP])
        pair = jnp.broadcast_to(two_lines(pair_ref, c), (8, STEP))
        value = jnp.zeros((8, STEP), F32)
        for k in range(QUADS):
            label = 2 * (2 * (k % (QUADS // 2)) + line // NOUT) + k // (QUADS // 2)
            value = value + jnp.where(label.astype(F32) == pair, g[8 * k : 8 * (k + 1), :], 0.0)
        value = (value + pltpu.roll(value, NOUT, 0)) * two_lines(area_ref, c)
        high = value.astype(BF16).astype(F32)
        both_ref[:, c * STEP : (c + 1) * STEP] = jnp.where(line < NOUT, high, value - high)
    for b in range(ROWS // BROWS):
        lanes = slice(b * BROWS, (b + 1) * BROWS)
        total = dot_nt(both_ref[:, lanes].astype(BF16), target_ref[:, lanes])
        atm_ref[:, BCOLS * b : BCOLS * (b + 1)] = total[:NOUT] + total[NOUT:]


def step_kernel(
    owner_hbm, forcing_hbm, sunlit_hbm, type_hbm, leaf_hbm, soil_hbm, table_hbm, area_hbm, column_hbm,
    atm_ref, after_hbm,
    owner_ref, forcing_ref, sunlit_ref, type_ref, leaf_ref, soil_ref, table_ref, area_ref, column_ref,
    in_sem, out_sem, send_sem, recv_sem,
    msg_ref, got_ref, reply_ref, home_ref,
    pair_ref, quad_ref, a_ref, split_ref, w_ref, lhs_ref, p_ref, early_ref, draw_ref, field_ref, flux_ref,
    both_ref,
):
    copies = [
        pltpu.make_async_copy(a, b, in_sem.at[i])
        for i, (a, b) in enumerate(
            (
                (owner_hbm, owner_ref), (forcing_hbm, forcing_ref), (sunlit_hbm, sunlit_ref),
                (type_hbm, type_ref), (leaf_hbm, leaf_ref), (soil_hbm, soil_ref),
                (table_hbm, table_ref), (area_hbm, area_ref), (column_hbm, column_ref),
            )
        )
    ]
    for copy in copies:
        copy.start()
    here = place()
    greet(here)
    copies[0].wait()
    copies[1].wait()
    pack(owner_ref, forcing_ref, msg_ref, pair_ref, a_ref, split_ref, w_ref)
    pl.semaphore_wait(pltpu.get_barrier_semaphore(), PEERS - 1)
    send_all(here, msg_ref, got_ref, SENT, send_sem.at[0], recv_sem.at[0])
    for copy in copies[2:]:
        copy.wait()
    prepare(sunlit_ref, type_ref, leaf_ref, table_ref, early_ref, draw_ref)
    await_all(msg_ref, got_ref, SENT, send_sem.at[0], recv_sem.at[0])
    unpack(got_ref, lhs_ref, p_ref, quad_ref, field_ref)
    physics(early_ref, field_ref, flux_ref)
    drain(soil_ref, draw_ref, flux_ref)
    reply(flux_ref, quad_ref, p_ref, w_ref, reply_ref)
    send_all(here, reply_ref, home_ref, BACK, send_sem.at[1], recv_sem.at[1])
    soil(soil_ref, draw_ref, field_ref, flux_ref)
    after = pltpu.make_async_copy(soil_ref, after_hbm, out_sem)
    after.start()
    targets(column_ref, a_ref)
    await_all(reply_ref, home_ref, BACK, send_sem.at[1], recv_sem.at[1])
    gather(home_ref, pair_ref, area_ref, split_ref, a_ref, atm_ref, both_ref)
    after.wait()


def hand_on_kernel(atm_ref, after_ref, atm_out, after_out, atm_buf, after_buf, in_sem, out_sem):
    pairs = [(atm_ref, atm_buf, atm_out)]
    for i in range(PARTS):
        lanes = pl.ds(i * (ROWS // PARTS), ROWS // PARTS)
        pairs.append(tuple(ref.at[:, lanes] for ref in (after_ref, after_buf, after_out)))
    inward = [pltpu.make_async_copy(a, b, in_sem.at[i]) for i, (a, b, _) in enumerate(pairs)]
    outward = [pltpu.make_async_copy(b, c, out_sem.at[i]) for i, (_, b, c) in enumerate(pairs)]
    for copy in inward:
        copy.start()
    for one, two in zip(inward, outward):
        one.wait()
        two.start()
    for copy in outward:
        copy.wait()


def body(forcing, owner, column, area, sunlit, plant_type, leaf_area, soil_water, pft_table):
    lines = lambda x: x.reshape(LINES, 128)
    i32 = jnp.int32
    flat = lambda dtype: pltpu.VMEM((LINES, 128), dtype)
    message = pltpu.VMEM((PEERS * 8, 128), F32)
    sem = pltpu.SemaphoreType.DMA
    atm_flux, soil_after = pl.pallas_call(
        step_kernel,
        out_shape=(
            jax.ShapeDtypeStruct((NOUT, ROWS // BROWS * BCOLS), F32),
            jax.ShapeDtypeStruct((LEVELS, ROWS), F32),
        ),
        in_specs=[pl.BlockSpec(memory_space=pl.ANY)] * 9,
        out_specs=(pl.BlockSpec(memory_space=pltpu.VMEM), pl.BlockSpec(memory_space=pl.ANY)),
        scratch_shapes=[
            flat(i32), pltpu.VMEM((NF, ROWS), BF16), flat(i32), flat(i32), flat(F32),
            pltpu.VMEM((LEVELS, ROWS), F32), pltpu.VMEM((4, NPFT), F32), flat(F32), flat(i32),
            sem((9,)), sem, sem((2,)), sem((2,)),
            message, message, message, message,
            flat(F32), flat(F32),
            pltpu.VMEM((PEERS, ROWS), BF16),
            pltpu.VMEM((2 * PEERS, ROWS), BF16),
            pltpu.VMEM((HALF + 16, ROWS), BF16),
            pltpu.VMEM((3, HALF // 2, STEP), BF16),
            pltpu.VMEM((4 * WINDOW, ROWS), BF16),
            pltpu.VMEM((6, LINES, 128), F32),
            pltpu.VMEM((16, ROWS), F32),
            pltpu.VMEM((LINES * NF, 128), F32),
            pltpu.VMEM((LINES * 8, 128), F32),
            pltpu.VMEM((8, ROWS), F32),
        ],
        compiler_params=pltpu.CompilerParams(
            collective_id=1, has_side_effects=True, vmem_limit_bytes=VMEM_LIMIT
        ),
        name="step",
    )(
        lines(owner), forcing, lines(sunlit), lines(plant_type), lines(leaf_area), soil_water, pft_table,
        lines(area), lines(column),
    )
    return pl.pallas_call(
        hand_on_kernel,
        out_shape=(
            jax.ShapeDtypeStruct(atm_flux.shape, F32),
            jax.ShapeDtypeStruct(soil_after.shape, F32),
        ),
        in_specs=[pl.BlockSpec(memory_space=pl.ANY)] * 2,
        out_specs=(pl.BlockSpec(memory_space=pl.ANY),) * 2,
        scratch_shapes=[
            pltpu.VMEM(atm_flux.shape, F32), pltpu.VMEM(soil_after.shape, F32), sem((PARTS + 1,)), sem((PARTS + 1,)),
        ],
        compiler_params=pltpu.CompilerParams(vmem_limit_bytes=VMEM_LIMIT),
        name="hand_on",
    )(atm_flux, soil_after)


def solution(mesh):
    spec = P(("row", "col"))
    wide = P(None, ("row", "col"))
    return jax.shard_map(
        body,
        mesh=mesh,
        in_specs=(wide, spec, spec, spec, spec, spec, spec, wide, P()),
        out_specs=(wide, wide),
        check_vma=False,
    )
```

```python
import jax
import jax.numpy as jnp
from jax import lax
from jax.experimental import pallas as pl
from jax.experimental.pallas import tpu as pltpu
from jax.sharding import PartitionSpec as P

NF = 8
NOUT = 4
NPFT = 16
LEVELS = 15
ITERS = 4
SOILP = 4
BROWS = 512
BCOLS = 128
PEERS = 128
ROWS = 8192
LINES = ROWS // 128
SLOTS = 80
QUADS = SLOTS // 4
STEP = 256
CHUNKS = ROWS // STEP
HALF = 2 * QUADS * NF
WINDOW = 64
SENT = NF * SLOTS // 128
BACK = 3
PARTS = 4
MESH = pl.DeviceIdType.MESH
F32 = jnp.float32
BF16 = jnp.bfloat16
NT = (((1,), (1,)), ((), ()))
VMEM_LIMIT = 56 * 1024 * 1024


def iota(shape, dim):
    return lax.broadcasted_iota(jnp.int32, shape, dim)


def as_bf16(mask):
    return jnp.where(mask, 1.0, 0.0).astype(BF16)


def dot(a, b):
    return jnp.dot(a, b, preferred_element_type=F32)


def dot_nt(a, b):
    return lax.dot_general(a, b, NT, preferred_element_type=F32)


def times_row(hot, row):
    rows, width = hot.shape
    tile = jnp.broadcast_to(row, (16, width)).astype(BF16)
    return (hot.reshape(rows // 16, 16, width) * tile[None]).reshape(rows, width)


def two_lines(ref, c):
    return jnp.concatenate([ref[2 * c : 2 * c + 1, :], ref[2 * c + 1 : 2 * c + 2, :]], axis=1)


def hops(step):
    return min(step, 4 - step)


OFFSETS = sorted(
    [(y, k, x, z) for y in range(4) for k in range(2) for x in range(4) for z in range(4)][1:],
    key=lambda o: -(3 * (hops(o[0]) + hops(o[2]) + hops(o[3])) + o[1]),
)


def place():
    row, col = lax.axis_index("row"), lax.axis_index("col")
    return row // 2, lax.rem(row, 2), col // 4, lax.rem(col, 4)


def neighbour(here, offset):
    y, k, x, z = (lax.rem(a + b, n) for a, b, n in zip(here, offset, (4, 2, 4, 4)))
    return y * 2 + k, x * 4 + z


def greet(here):
    barrier = pltpu.get_barrier_semaphore()
    for offset in OFFSETS:
        pl.semaphore_signal(barrier, inc=1, device_id=neighbour(here, offset), device_id_type=MESH)


def slot_of(ref, index, lines):
    if ref.dtype == BF16:
        return ref.at[index]
    return ref.at[pl.ds(pl.multiple_of(index * 8, 8), lines), :]


def send_all(here, msg_ref, got_ref, lines, send_sem, recv_sem):
    row, col = neighbour(here, (0, 0, 0, 0))
    me = row * 16 + col
    for offset in OFFSETS:
        row, col = neighbour(here, offset)
        pltpu.make_async_remote_copy(
            src_ref=slot_of(msg_ref, row * 16 + col, lines),
            dst_ref=slot_of(got_ref, me, lines),
            send_sem=send_sem,
            recv_sem=recv_sem,
            device_id=(row, col),
            device_id_type=MESH,
        ).start()
    pltpu.make_async_copy(slot_of(msg_ref, me, lines), slot_of(got_ref, me, lines), recv_sem).start()


def await_all(msg_ref, got_ref, lines, send_sem, recv_sem):
    unit = 1 if msg_ref.dtype == BF16 else lines
    sent = msg_ref.at[: (PEERS - 1) * unit]
    pltpu.make_async_copy(sent, sent, send_sem).wait()
    got = got_ref.at[: PEERS * unit]
    pltpu.make_async_copy(got, got, recv_sem).wait()


def fold(lines, flat_ref):
    for i, line in enumerate(lines):
        flat_ref[pl.ds(i, PEERS, stride=8), :] = line


def unfold(flat_ref, lines):
    return jnp.concatenate([flat_ref[pl.ds(i, PEERS, stride=8), :].T for i in range(lines)], axis=0)


def pack(owner_ref, forcing_ref, flat_ref, msg_ref, pair_ref, a_ref, split_ref, w_ref):
    ids = iota((PEERS, 128), 0)
    for j in range(LINES):
        a_ref[:, 128 * j : 128 * (j + 1)] = as_bf16(ids == owner_ref[j : j + 1, :])
    upto = as_bf16(iota((STEP, STEP), 0) <= iota((STEP, STEP), 1))
    base = jnp.zeros((PEERS, 1), F32)
    for c in range(CHUNKS):
        a = a_ref[:, c * STEP : (c + 1) * STEP]
        seen = dot(a, upto)
        mine = (seen + base).astype(BF16) * a
        base = base + seen[:, STEP - 1 :]
        mine = mine.reshape(PEERS // 16, 16, STEP)
        total = mine[0]
        for i in range(1, PEERS // 16):
            total = total + mine[i]
        rank = jnp.sum(total.astype(F32), axis=0, keepdims=True) - 1.0
        pair = jnp.floor(rank * 0.5)
        odd = rank - 2.0 * pair
        pair_ref[2 * c : 2 * c + 1, :] = pair[:, :128]
        pair_ref[2 * c + 1 : 2 * c + 2, :] = pair[:, 128:]
        split_ref[:PEERS, c * STEP : (c + 1) * STEP] = times_row(a, 1.0 - odd)
        split_ref[PEERS:, c * STEP : (c + 1) * STEP] = times_row(a, odd)
    line = iota((16, STEP), 0)
    for c in range(CHUNKS):
        pair = jnp.broadcast_to(two_lines(pair_ref, c), (16, STEP)).astype(BF16)
        x = forcing_ref[:, c * STEP : (c + 1) * STEP].astype(F32)
        x = jnp.concatenate([x, x], axis=0).astype(BF16)
        for k in range(2 * QUADS // 2):
            label = 2 * (2 * (k % (QUADS // 2)) + line // 8) + k // (QUADS // 2)
            hit = label.astype(F32).astype(BF16) == pair
            w_ref[16 * k : 16 * (k + 1), c * STEP : (c + 1) * STEP] = jnp.where(hit, x, jnp.zeros((), BF16))
    w_ref[HALF:, :] = jnp.ones((16, ROWS), BF16)
    got = dot_nt(w_ref[...], split_ref[...])
    counts = got[HALF : HALF + 1, :PEERS] + got[HALF : HALF + 1, PEERS:]
    line = iota((HALF, PEERS), 0)
    label = 4 * (lax.rem(line, HALF // 2) // NF) + 2 * (line // (HALF // 2))
    values = [
        jnp.where((label + odd).astype(F32) < counts, got[:HALF, PEERS * odd : PEERS * (odd + 1)], -1.0)
        for odd in range(2)
    ]
    values = jnp.concatenate(values, axis=0)
    lines = [values[128 * i : 128 * (i + 1), :].T for i in range(SENT)]
    fold(lines + [jnp.zeros((PEERS, 128), F32)], flat_ref)
    msg_ref[...] = flat_ref[...].reshape(PEERS, 8, 128)[:, : SENT + 1].astype(BF16)


def look(row, kinds):
    return jnp.take_along_axis(jnp.broadcast_to(row, kinds.shape), kinds, axis=1, mode="promise_in_bounds")


def prepare(sunlit_ref, type_ref, leaf_ref, table_ref, early_ref, draw_ref):
    table = jnp.concatenate([table_ref[...], jnp.zeros((4, 128 - NPFT), F32)], axis=1)
    single_t = jnp.sqrt(1.0 - (0.1 + 0.3 * table[0:1]))
    reflect_t = (1.0 - single_t) / (1.0 + single_t)
    kroot_t = 0.05 + 0.5 * table[3:4]
    level = iota((16, 128), 0)
    roots_t = jnp.where(level < LEVELS, jnp.exp(-kroot_t * level.astype(F32)), 0.0)
    roots_t = 0.05 * (roots_t / jnp.sum(roots_t, axis=0, keepdims=True))
    kinds = type_ref[...]
    leaf = leaf_ref[...]
    single = look(single_t, kinds)
    reflect_h = look(reflect_t, kinds)
    lit = sunlit_ref[...].astype(F32)
    early_ref[0] = single * leaf
    early_ref[1] = reflect_h
    early_ref[2] = look(0.5 + 1.5 * table[1:2], kinds)
    early_ref[3] = look(3.0 + 6.0 * table[2:3], kinds)
    early_ref[4] = lit
    early_ref[5] = lit * (1.0 - reflect_h) * (1.0 - jnp.exp(-0.8 * single * leaf))
    for j in range(LINES):
        draw_ref[:, 128 * j : 128 * (j + 1)] = look(roots_t, jnp.broadcast_to(type_ref[j : j + 1, :], (16, 128)))


def window_of(c):
    least = c * STEP // SLOTS
    most = min(PEERS - 1, (PEERS * SLOTS - ROWS + c * STEP + STEP - 1) // SLOTS)
    for w in range(3):
        if 32 * w <= least and most < 32 * w + WINDOW:
            return w
    raise ValueError


def arrange(got_ref, flat_ref, lhs_ref):
    got = jnp.concatenate([got_ref[...].astype(F32), jnp.zeros((PEERS, 2, 128), F32)], axis=1)
    flat_ref[...] = got.reshape(PEERS * 8, 128)
    got = unfold(flat_ref, SENT)
    valid = jnp.where(got >= 0.0, 1.0 / NF, 0.0)
    counts = jnp.sum(valid, axis=0, keepdims=True)
    part = lambda odd, a: got[HALF * odd + HALF // 2 * a : HALF * odd + HALF // 2 * (a + 1), :]
    low = iota((HALF // 2, 128), 1) < WINDOW
    for a in range(2):
        even, odd = part(0, a), part(1, a)
        for w in range(3):
            left = even if w == 0 else pltpu.roll(even, 128 - 32 * w, 1)
            right = odd if w == 2 else pltpu.roll(odd, 64 - 32 * w, 1)
            lhs_ref[w, :, 128 * a : 128 * (a + 1)] = jnp.where(low, left, right).astype(BF16)
    before = iota((PEERS, PEERS), 1) < iota((PEERS, PEERS), 0)
    upto = iota((PEERS, PEERS), 1) <= iota((PEERS, PEERS), 0)
    ones = jnp.ones((PEERS, STEP), BF16)
    begin = dot(jnp.where(before, counts, 0.0).astype(BF16), ones)
    end = dot(jnp.where(upto, counts, 0.0).astype(BF16), ones)
    return begin, end


def unpack(got_ref, flat_ref, lhs_ref, p_ref, quad_ref, field_ref):
    begin, end = arrange(got_ref, flat_ref, lhs_ref)
    for c in range(CHUNKS):
        w = window_of(c)
        first = begin[32 * w : 32 * w + WINDOW]
        tile = (iota((1, STEP), 1) + c * STEP).astype(F32)
        mine = (tile >= first) & (tile < end[32 * w : 32 * w + WINDOW])
        slot = tile - jnp.sum(jnp.where(mine, first, 0.0), axis=0, keepdims=True)
        quad = jnp.floor(slot * 0.25)
        rest = slot - 4.0 * quad
        quad_ref[2 * c : 2 * c + 1, :] = quad[:, :128]
        quad_ref[2 * c + 1 : 2 * c + 2, :] = quad[:, 128:]
        hot = as_bf16(mine)
        for k in range(4):
            p_ref[WINDOW * k : WINDOW * (k + 1), c * STEP : (c + 1) * STEP] = times_row(
                hot, jnp.where(rest == float(k), 1.0, 0.0)
            )
    for c in range(CHUNKS):
        g = dot(lhs_ref[window_of(c)], p_ref[:, c * STEP : (c + 1) * STEP])
        quad = jnp.broadcast_to(two_lines(quad_ref, c), (NF, STEP))
        value = jnp.zeros((NF, STEP), F32)
        for s in range(QUADS):
            value = value + jnp.where(quad == float(s), g[NF * s : NF * (s + 1), :], 0.0)
        field_ref[NF * 2 * c : NF * (2 * c + 1), :] = value[:, :128]
        field_ref[NF * (2 * c + 1) : NF * (2 * c + 2), :] = value[:, 128:]


def physics(early_ref, field_ref, flux_ref):
    field = lambda f: field_ref[pl.ds(f, LINES, stride=NF), :]
    thick, reflect_h, vcmax, slope, lit, diffuse = (early_ref[i] for i in range(6))
    swdir = 2.0 * field(0)
    tair = field(2) - 0.5
    vapour = 0.2 + field(3)
    carbon = 0.8 + 0.4 * field(4)
    coszen = 0.1 + 0.9 * field(5)
    wind_speed = 0.5 + 2.0 * field(6)
    extinct = 0.5 / coszen
    reflect_b = 2.0 * extinct * reflect_h / (1.0 + extinct)
    light = lit * (1.0 - reflect_b) * swdir * (1.0 - jnp.exp(-extinct * thick)) + diffuse * field(1)
    electrons = 0.3 * light
    compensation = 0.08 * (1.0 + 0.3 * tair)
    capacity_t = vcmax * jnp.exp(0.5 * tair)
    internal = 0.7 * carbon
    for repeat in range(ITERS):
        limit = internal - compensation
        carboxyl = capacity_t * limit / (internal + 0.6)
        ribulose = electrons * limit / (4.0 * internal + 8.0 * compensation)
        assim = carboxyl * ribulose / (carboxyl + ribulose)
        conduct = 0.05 + slope * assim / carbon
        internal = carbon - 1.6 * assim / conduct
    transpire = conduct * vapour
    for f, value in enumerate((assim, transpire, 0.5 * wind_speed * (0.2 * light - 0.5 * transpire))):
        flux_ref[pl.ds(f, LINES, stride=8), :] = value
        flux_ref[pl.ds(f + NOUT, LINES, stride=8), :] = value


def soil_pass(theta, draw, level):
    above = jnp.where(level == 0, theta, pltpu.roll(theta, 1, 0))
    under = jnp.where(level == LEVELS - 1, theta, pltpu.roll(theta, theta.shape[0] - 1, 0))
    return theta + 0.25 * (above + under - 2.0 * theta) - draw


def drain(soil_ref, draw_ref, flux_ref):
    level = iota((8, 128), 0) + 8
    for j in range(LINES):
        lanes = slice(128 * j, 128 * (j + 1))
        draw = draw_ref[8:, lanes] * flux_ref[8 * j + 1 : 8 * j + 2, :]
        theta = jnp.concatenate([soil_ref[8:, lanes], jnp.zeros((1, 128), F32)], axis=0)
        for repeat in range(SOILP):
            theta = soil_pass(theta, draw, level)
        value = 0.5 * theta[LEVELS - 9 : LEVELS - 8, :]
        flux_ref[8 * j + 3 : 8 * j + 4, :] = value
        flux_ref[8 * j + 7 : 8 * j + 8, :] = value


def soil(soil_ref, draw_ref, field_ref, flux_ref):
    level = iota((16, 128), 0)
    for j in range(LINES):
        lanes = slice(128 * j, 128 * (j + 1))
        draw = draw_ref[:, lanes] * flux_ref[8 * j + 1 : 8 * j + 2, :]
        theta = jnp.concatenate([soil_ref[:, lanes], jnp.zeros((1, 128), F32)], axis=0)
        theta = theta + jnp.where(level == 0, 0.1 * field_ref[NF * j + 7 : NF * j + 8, :], 0.0)
        for repeat in range(SOILP):
            theta = soil_pass(theta, draw, level)
        soil_ref[:, lanes] = theta[:LEVELS]


def reply(flux_ref, quad_ref, p_ref, w_ref, msg_ref):
    line = iota((8, 128), 0)
    for j in range(LINES):
        flux = flux_ref[8 * j : 8 * (j + 1), :]
        quad = jnp.broadcast_to(quad_ref[j : j + 1, :], (8, 128))
        parts = [
            jnp.where((2 * k + line // NOUT).astype(F32) == quad, flux, 0.0) for k in range(QUADS // 2)
        ]
        w_ref[: NOUT * QUADS, 128 * j : 128 * (j + 1)] = jnp.concatenate(parts, axis=0).astype(BF16)
    held = []
    for w in range(3):
        mine = [c for c in range(CHUNKS) if window_of(c) == w]
        lanes = slice(mine[0] * STEP, (mine[-1] + 1) * STEP)
        held.append(dot_nt(p_ref[:, lanes], w_ref[: NOUT * QUADS, lanes]))
    parts = []
    for k in range(4):
        a, b, c = (g[WINDOW * k : WINDOW * (k + 1)] for g in held)
        rows = jnp.concatenate([a[:32], a[32:] + b[:32], b[32:] + c[:32], c[32:]], axis=0)
        rows = jnp.concatenate([rows, jnp.zeros((PEERS, 128 - NOUT * QUADS), F32)], axis=1)
        shift = NOUT * QUADS * k % 128
        parts.append(pltpu.roll(rows, shift, 1) if shift else rows)
    lane = iota((PEERS, 128), 1)
    lines = (
        jnp.where(lane < 80, parts[0], parts[1]),
        jnp.where(lane < 32, parts[1], jnp.where(lane < 112, parts[2], parts[3])),
        parts[3],
    )
    fold(lines, msg_ref)


def targets(column_ref, target_ref):
    ids = iota((BCOLS, 128), 0)
    for j in range(LINES):
        target_ref[:, 128 * j : 128 * (j + 1)] = as_bf16(ids == column_ref[j : j + 1, :])


def gather(home_ref, pair_ref, area_ref, split_ref, target_ref, atm_ref, both_ref):
    got = unfold(home_ref, BACK)
    rows = NOUT * QUADS
    part = lambda k: got[rows * k : rows * (k + 1), :]
    even = jnp.concatenate([part(0), part(2)], axis=0)
    odd = jnp.concatenate([part(1), part(3)], axis=0)
    lhs = jnp.concatenate([even, odd], axis=1).astype(BF16)
    line = iota((8, STEP), 0)
    for c in range(CHUNKS):
        g = dot(lhs, split_ref[:, c * STEP : (c + 1) * STEP])
        pair = jnp.broadcast_to(two_lines(pair_ref, c), (8, STEP))
        value = jnp.zeros((8, STEP), F32)
        for k in range(QUADS):
            label = 2 * (2 * (k % (QUADS // 2)) + line // NOUT) + k // (QUADS // 2)
            value = value + jnp.where(label.astype(F32) == pair, g[8 * k : 8 * (k + 1), :], 0.0)
        value = (value + pltpu.roll(value, NOUT, 0)) * two_lines(area_ref, c)
        high = value.astype(BF16).astype(F32)
        both_ref[:, c * STEP : (c + 1) * STEP] = jnp.where(line < NOUT, high, value - high)
    for b in range(ROWS // BROWS):
        lanes = slice(b * BROWS, (b + 1) * BROWS)
        total = dot_nt(both_ref[:, lanes].astype(BF16), target_ref[:, lanes])
        atm_ref[:, BCOLS * b : BCOLS * (b + 1)] = total[:NOUT] + total[NOUT:]


def step_kernel(
    owner_hbm, forcing_hbm, sunlit_hbm, type_hbm, leaf_hbm, soil_hbm, table_hbm, area_hbm, column_hbm,
    atm_ref, after_hbm,
    owner_ref, forcing_ref, sunlit_ref, type_ref, leaf_ref, soil_ref, table_ref, area_ref, column_ref,
    in_sem, out_sem, send_sem, recv_sem,
    msg_ref, got_ref, reply_ref, home_ref, flat_ref,
    pair_ref, quad_ref, a_ref, split_ref, w_ref, lhs_ref, p_ref, early_ref, draw_ref, field_ref, flux_ref,
    both_ref,
):
    copies = [
        pltpu.make_async_copy(a, b, in_sem.at[i])
        for i, (a, b) in enumerate(
            (
                (owner_hbm, owner_ref), (forcing_hbm, forcing_ref), (sunlit_hbm, sunlit_ref),
                (type_hbm, type_ref), (leaf_hbm, leaf_ref), (soil_hbm, soil_ref),
                (table_hbm, table_ref), (area_hbm, area_ref), (column_hbm, column_ref),
            )
        )
    ]
    for copy in copies:
        copy.start()
    here = place()
    greet(here)
    copies[0].wait()
    copies[1].wait()
    pack(owner_ref, forcing_ref, flat_ref, msg_ref, pair_ref, a_ref, split_ref, w_ref)
    pl.semaphore_wait(pltpu.get_barrier_semaphore(), PEERS - 1)
    send_all(here, msg_ref, got_ref, SENT, send_sem.at[0], recv_sem.at[0])
    for copy in copies[2:]:
        copy.wait()
    prepare(sunlit_ref, type_ref, leaf_ref, table_ref, early_ref, draw_ref)
    await_all(msg_ref, got_ref, SENT, send_sem.at[0], recv_sem.at[0])
    unpack(got_ref, flat_ref, lhs_ref, p_ref, quad_ref, field_ref)
    physics(early_ref, field_ref, flux_ref)
    drain(soil_ref, draw_ref, flux_ref)
    reply(flux_ref, quad_ref, p_ref, w_ref, reply_ref)
    send_all(here, reply_ref, home_ref, BACK, send_sem.at[1], recv_sem.at[1])
    soil(soil_ref, draw_ref, field_ref, flux_ref)
    after = pltpu.make_async_copy(soil_ref, after_hbm, out_sem)
    after.start()
    targets(column_ref, a_ref)
    await_all(reply_ref, home_ref, BACK, send_sem.at[1], recv_sem.at[1])
    gather(home_ref, pair_ref, area_ref, split_ref, a_ref, atm_ref, both_ref)
    after.wait()


def hand_on_kernel(atm_ref, after_ref, atm_out, after_out, atm_buf, after_buf, in_sem, out_sem):
    pairs = [(atm_ref, atm_buf, atm_out)]
    for i in range(PARTS):
        lanes = pl.ds(i * (ROWS // PARTS), ROWS // PARTS)
        pairs.append(tuple(ref.at[:, lanes] for ref in (after_ref, after_buf, after_out)))
    inward = [pltpu.make_async_copy(a, b, in_sem.at[i]) for i, (a, b, _) in enumerate(pairs)]
    outward = [pltpu.make_async_copy(b, c, out_sem.at[i]) for i, (_, b, c) in enumerate(pairs)]
    for copy in inward:
        copy.start()
    for one, two in zip(inward, outward):
        one.wait()
        two.start()
    for copy in outward:
        copy.wait()


def body(forcing, owner, column, area, sunlit, plant_type, leaf_area, soil_water, pft_table):
    lines = lambda x: x.reshape(LINES, 128)
    i32 = jnp.int32
    flat = lambda dtype: pltpu.VMEM((LINES, 128), dtype)
    there = pltpu.VMEM((PEERS, SENT + 1, 128), BF16)
    back = pltpu.VMEM((PEERS * 8, 128), F32)
    sem = pltpu.SemaphoreType.DMA
    atm_flux, soil_after = pl.pallas_call(
        step_kernel,
        out_shape=(
            jax.ShapeDtypeStruct((NOUT, ROWS // BROWS * BCOLS), F32),
            jax.ShapeDtypeStruct((LEVELS, ROWS), F32),
        ),
        in_specs=[pl.BlockSpec(memory_space=pl.ANY)] * 9,
        out_specs=(pl.BlockSpec(memory_space=pltpu.VMEM), pl.BlockSpec(memory_space=pl.ANY)),
        scratch_shapes=[
            flat(i32), pltpu.VMEM((NF, ROWS), BF16), flat(i32), flat(i32), flat(F32),
            pltpu.VMEM((LEVELS, ROWS), F32), pltpu.VMEM((4, NPFT), F32), flat(F32), flat(i32),
            sem((9,)), sem, sem((2,)), sem((2,)),
            there, there, back, back, back,
            flat(F32), flat(F32),
            pltpu.VMEM((PEERS, ROWS), BF16),
            pltpu.VMEM((2 * PEERS, ROWS), BF16),
            pltpu.VMEM((HALF + 16, ROWS), BF16),
            pltpu.VMEM((3, HALF // 2, STEP), BF16),
            pltpu.VMEM((4 * WINDOW, ROWS), BF16),
            pltpu.VMEM((6, LINES, 128), F32),
            pltpu.VMEM((16, ROWS), F32),
            pltpu.VMEM((LINES * NF, 128), F32),
            pltpu.VMEM((LINES * 8, 128), F32),
            pltpu.VMEM((8, ROWS), F32),
        ],
        compiler_params=pltpu.CompilerParams(
            collective_id=1, has_side_effects=True, vmem_limit_bytes=VMEM_LIMIT
        ),
        name="step",
    )(
        lines(owner), forcing, lines(sunlit), lines(plant_type), lines(leaf_area), soil_water, pft_table,
        lines(area), lines(column),
    )
    return pl.pallas_call(
        hand_on_kernel,
        out_shape=(
            jax.ShapeDtypeStruct(atm_flux.shape, F32),
            jax.ShapeDtypeStruct(soil_after.shape, F32),
        ),
        in_specs=[pl.BlockSpec(memory_space=pl.ANY)] * 2,
        out_specs=(pl.BlockSpec(memory_space=pl.ANY),) * 2,
        scratch_shapes=[
            pltpu.VMEM(atm_flux.shape, F32), pltpu.VMEM(soil_after.shape, F32), sem((PARTS + 1,)), sem((PARTS + 1,)),
        ],
        compiler_params=pltpu.CompilerParams(vmem_limit_bytes=VMEM_LIMIT),
        name="hand_on",
    )(atm_flux, soil_after)


def solution(mesh):
    spec = P(("row", "col"))
    wide = P(None, ("row", "col"))
    return jax.shard_map(
        body,
        mesh=mesh,
        in_specs=(wide, spec, spec, spec, spec, spec, spec, wide, P()),
        out_specs=(wide, wide),
        check_vma=False,
    )
```

```python
import jax
import jax.numpy as jnp
from jax import lax
from jax.experimental import pallas as pl
from jax.experimental.pallas import tpu as pltpu
from jax.sharding import PartitionSpec as P

NF = 8
NOUT = 4
NPFT = 16
LEVELS = 15
ITERS = 4
SOILP = 4
BROWS = 512
BCOLS = 128
PEERS = 128
ROWS = 8192
LINES = ROWS // 128
SLOTS = 80
QUADS = SLOTS // 4
STEP = 256
CHUNKS = ROWS // STEP
HALF = 2 * QUADS * NF
WINDOW = 64
SENT = NF * SLOTS // 128
BACK = 3
PARTS = 4
MESH = pl.DeviceIdType.MESH
F32 = jnp.float32
BF16 = jnp.bfloat16
NT = (((1,), (1,)), ((), ()))
VMEM_LIMIT = 56 * 1024 * 1024


def iota(shape, dim):
    return lax.broadcasted_iota(jnp.int32, shape, dim)


def as_bf16(mask):
    return jnp.where(mask, 1.0, 0.0).astype(BF16)


def dot(a, b):
    return jnp.dot(a, b, preferred_element_type=F32)


def dot_nt(a, b):
    return lax.dot_general(a, b, NT, preferred_element_type=F32)


def times_row(hot, row):
    rows, width = hot.shape
    tile = jnp.broadcast_to(row, (16, width)).astype(BF16)
    return (hot.reshape(rows // 16, 16, width) * tile[None]).reshape(rows, width)


def two_lines(ref, c):
    return jnp.concatenate([ref[2 * c : 2 * c + 1, :], ref[2 * c + 1 : 2 * c + 2, :]], axis=1)


def hops(step):
    return min(step, 4 - step)


OFFSETS = sorted(
    [(y, k, x, z) for y in range(4) for k in range(2) for x in range(4) for z in range(4)][1:],
    key=lambda o: -(3 * (hops(o[0]) + hops(o[2]) + hops(o[3])) + o[1]),
)


def place():
    row, col = lax.axis_index("row"), lax.axis_index("col")
    return row // 2, lax.rem(row, 2), col // 4, lax.rem(col, 4)


def neighbour(here, offset):
    y, k, x, z = (lax.rem(a + b, n) for a, b, n in zip(here, offset, (4, 2, 4, 4)))
    return y * 2 + k, x * 4 + z


def greet(here):
    barrier = pltpu.get_barrier_semaphore()
    for offset in OFFSETS:
        pl.semaphore_signal(barrier, inc=1, device_id=neighbour(here, offset), device_id_type=MESH)


def slot_of(ref, index, lines):
    if ref.dtype == BF16:
        return ref.at[index]
    return ref.at[pl.ds(pl.multiple_of(index * 8, 8), lines), :]


def send_all(here, msg_ref, got_ref, lines, send_sem, recv_sem):
    row, col = neighbour(here, (0, 0, 0, 0))
    me = row * 16 + col
    for offset in OFFSETS:
        row, col = neighbour(here, offset)
        pltpu.make_async_remote_copy(
            src_ref=slot_of(msg_ref, row * 16 + col, lines),
            dst_ref=slot_of(got_ref, me, lines),
            send_sem=send_sem,
            recv_sem=recv_sem,
            device_id=(row, col),
            device_id_type=MESH,
        ).start()
    pltpu.make_async_copy(slot_of(msg_ref, me, lines), slot_of(got_ref, me, lines), recv_sem).start()


def await_all(msg_ref, got_ref, lines, send_sem, recv_sem):
    unit = 1 if msg_ref.dtype == BF16 else lines
    sent = msg_ref.at[: (PEERS - 1) * unit]
    pltpu.make_async_copy(sent, sent, send_sem).wait()
    got = got_ref.at[: PEERS * unit]
    pltpu.make_async_copy(got, got, recv_sem).wait()


def fold(lines, flat_ref):
    for i, line in enumerate(lines):
        flat_ref[pl.ds(i, PEERS, stride=8), :] = line


def unfold(flat_ref, lines):
    return jnp.concatenate([flat_ref[pl.ds(i, PEERS, stride=8), :].T for i in range(lines)], axis=0)


def pack(owner_ref, forcing_ref, flat_ref, msg_ref, pair_ref, a_ref, split_ref, w_ref):
    ids = iota((PEERS, 128), 0)
    for j in range(LINES):
        a_ref[:, 128 * j : 128 * (j + 1)] = as_bf16(ids == owner_ref[j : j + 1, :])
    upto = as_bf16(iota((STEP, STEP), 0) <= iota((STEP, STEP), 1))
    base = jnp.zeros((PEERS, 1), F32)
    for c in range(CHUNKS):
        a = a_ref[:, c * STEP : (c + 1) * STEP]
        seen = dot(a, upto)
        mine = (seen + base).astype(BF16) * a
        base = base + seen[:, STEP - 1 :]
        mine = mine.reshape(PEERS // 16, 16, STEP)
        total = mine[0]
        for i in range(1, PEERS // 16):
            total = total + mine[i]
        rank = jnp.sum(total.astype(F32), axis=0, keepdims=True) - 1.0
        pair = jnp.floor(rank * 0.5)
        odd = rank - 2.0 * pair
        pair_ref[2 * c : 2 * c + 1, :] = pair[:, :128]
        pair_ref[2 * c + 1 : 2 * c + 2, :] = pair[:, 128:]
        split_ref[:PEERS, c * STEP : (c + 1) * STEP] = times_row(a, 1.0 - odd)
        split_ref[PEERS:, c * STEP : (c + 1) * STEP] = times_row(a, odd)
    line = iota((16, STEP), 0)
    for c in range(CHUNKS):
        pair = jnp.broadcast_to(two_lines(pair_ref, c), (16, STEP)).astype(BF16)
        x = forcing_ref[:, c * STEP : (c + 1) * STEP].astype(F32)
        x = jnp.concatenate([x, x], axis=0).astype(BF16)
        for k in range(2 * QUADS // 2):
            label = 2 * (2 * (k % (QUADS // 2)) + line // 8) + k // (QUADS // 2)
            hit = label.astype(F32).astype(BF16) == pair
            w_ref[16 * k : 16 * (k + 1), c * STEP : (c + 1) * STEP] = jnp.where(hit, x, jnp.zeros((), BF16))
    w_ref[HALF:, :] = jnp.ones((16, ROWS), BF16)
    got = dot_nt(w_ref[...], split_ref[...])
    counts = got[HALF : HALF + 1, :PEERS] + got[HALF : HALF + 1, PEERS:]
    line = iota((HALF, PEERS), 0)
    label = 4 * (lax.rem(line, HALF // 2) // NF) + 2 * (line // (HALF // 2))
    values = [
        jnp.where((label + odd).astype(F32) < counts, got[:HALF, PEERS * odd : PEERS * (odd + 1)], -1.0)
        for odd in range(2)
    ]
    values = jnp.concatenate(values, axis=0)
    lines = [values[128 * i : 128 * (i + 1), :].T for i in range(SENT)]
    fold(lines + [jnp.zeros((PEERS, 128), F32)], flat_ref)
    msg_ref[...] = flat_ref[: PEERS * 8, :].reshape(PEERS, 8, 128)[:, : SENT + 1].astype(BF16)


def look(row, kinds):
    return jnp.take_along_axis(jnp.broadcast_to(row, kinds.shape), kinds, axis=1, mode="promise_in_bounds")


def prepare(sunlit_ref, type_ref, leaf_ref, table_ref, early_ref, draw_ref):
    table = jnp.concatenate([table_ref[...], jnp.zeros((4, 128 - NPFT), F32)], axis=1)
    single_t = jnp.sqrt(1.0 - (0.1 + 0.3 * table[0:1]))
    reflect_t = (1.0 - single_t) / (1.0 + single_t)
    kroot_t = 0.05 + 0.5 * table[3:4]
    level = iota((16, 128), 0)
    roots_t = jnp.where(level < LEVELS, jnp.exp(-kroot_t * level.astype(F32)), 0.0)
    roots_t = 0.05 * (roots_t / jnp.sum(roots_t, axis=0, keepdims=True))
    kinds = type_ref[...]
    leaf = leaf_ref[...]
    single = look(single_t, kinds)
    reflect_h = look(reflect_t, kinds)
    lit = sunlit_ref[...].astype(F32)
    early_ref[0] = single * leaf
    early_ref[1] = reflect_h
    early_ref[2] = look(0.5 + 1.5 * table[1:2], kinds)
    early_ref[3] = look(3.0 + 6.0 * table[2:3], kinds)
    early_ref[4] = lit
    early_ref[5] = lit * (1.0 - reflect_h) * (1.0 - jnp.exp(-0.8 * single * leaf))
    for j in range(LINES):
        draw_ref[:, 128 * j : 128 * (j + 1)] = look(roots_t, jnp.broadcast_to(type_ref[j : j + 1, :], (16, 128)))


def window_of(c):
    least = c * STEP // SLOTS
    most = min(PEERS - 1, (PEERS * SLOTS - ROWS + c * STEP + STEP - 1) // SLOTS)
    for w in range(3):
        if 32 * w <= least and most < 32 * w + WINDOW:
            return w
    raise ValueError


def arrange(got_ref, flat_ref, lhs_ref):
    got = jnp.concatenate([got_ref[...].astype(F32), jnp.zeros((PEERS, 2, 128), F32)], axis=1)
    flat_ref[: PEERS * 8, :] = got.reshape(PEERS * 8, 128)
    got = unfold(flat_ref, SENT)
    valid = jnp.where(got >= 0.0, 1.0 / NF, 0.0)
    counts = jnp.sum(valid, axis=0, keepdims=True)
    part = lambda odd, a: got[HALF * odd + HALF // 2 * a : HALF * odd + HALF // 2 * (a + 1), :]
    low = iota((HALF // 2, 128), 1) < WINDOW
    for a in range(2):
        even, odd = part(0, a), part(1, a)
        for w in range(3):
            left = even if w == 0 else pltpu.roll(even, 128 - 32 * w, 1)
            right = odd if w == 2 else pltpu.roll(odd, 64 - 32 * w, 1)
            lhs_ref[w, :, 128 * a : 128 * (a + 1)] = jnp.where(low, left, right).astype(BF16)
    before = iota((PEERS, PEERS), 1) < iota((PEERS, PEERS), 0)
    upto = iota((PEERS, PEERS), 1) <= iota((PEERS, PEERS), 0)
    ones = jnp.ones((PEERS, STEP), BF16)
    begin = dot(jnp.where(before, counts, 0.0).astype(BF16), ones)
    end = dot(jnp.where(upto, counts, 0.0).astype(BF16), ones)
    return begin, end


def unpack(got_ref, flat_ref, lhs_ref, p_ref, quad_ref, field_ref):
    begin, end = arrange(got_ref, flat_ref, lhs_ref)
    for c in range(CHUNKS):
        w = window_of(c)
        first = begin[32 * w : 32 * w + WINDOW]
        tile = (iota((1, STEP), 1) + c * STEP).astype(F32)
        mine = (tile >= first) & (tile < end[32 * w : 32 * w + WINDOW])
        slot = tile - jnp.sum(jnp.where(mine, first, 0.0), axis=0, keepdims=True)
        quad = jnp.floor(slot * 0.25)
        rest = slot - 4.0 * quad
        quad_ref[2 * c : 2 * c + 1, :] = quad[:, :128]
        quad_ref[2 * c + 1 : 2 * c + 2, :] = quad[:, 128:]
        hot = as_bf16(mine)
        for k in range(4):
            p_ref[WINDOW * k : WINDOW * (k + 1), c * STEP : (c + 1) * STEP] = times_row(
                hot, jnp.where(rest == float(k), 1.0, 0.0)
            )
    for c in range(CHUNKS):
        g = dot(lhs_ref[window_of(c)], p_ref[:, c * STEP : (c + 1) * STEP])
        quad = jnp.broadcast_to(two_lines(quad_ref, c), (NF, STEP))
        value = jnp.zeros((NF, STEP), F32)
        for s in range(QUADS):
            value = value + jnp.where(quad == float(s), g[NF * s : NF * (s + 1), :], 0.0)
        field_ref[NF * 2 * c : NF * (2 * c + 1), :] = value[:, :128]
        field_ref[NF * (2 * c + 1) : NF * (2 * c + 2), :] = value[:, 128:]


def physics(early_ref, field_ref, flux_ref):
    field = lambda f: field_ref[pl.ds(f, LINES, stride=NF), :]
    thick, reflect_h, vcmax, slope, lit, diffuse = (early_ref[i] for i in range(6))
    swdir = 2.0 * field(0)
    tair = field(2) - 0.5
    vapour = 0.2 + field(3)
    carbon = 0.8 + 0.4 * field(4)
    coszen = 0.1 + 0.9 * field(5)
    wind_speed = 0.5 + 2.0 * field(6)
    extinct = 0.5 / coszen
    reflect_b = 2.0 * extinct * reflect_h / (1.0 + extinct)
    light = lit * (1.0 - reflect_b) * swdir * (1.0 - jnp.exp(-extinct * thick)) + diffuse * field(1)
    electrons = 0.3 * light
    compensation = 0.08 * (1.0 + 0.3 * tair)
    capacity_t = vcmax * jnp.exp(0.5 * tair)
    internal = 0.7 * carbon
    for repeat in range(ITERS):
        limit = internal - compensation
        carboxyl = capacity_t * limit / (internal + 0.6)
        ribulose = electrons * limit / (4.0 * internal + 8.0 * compensation)
        assim = carboxyl * ribulose / (carboxyl + ribulose)
        conduct = 0.05 + slope * assim / carbon
        internal = carbon - 1.6 * assim / conduct
    transpire = conduct * vapour
    for f, value in enumerate((assim, transpire, 0.5 * wind_speed * (0.2 * light - 0.5 * transpire))):
        flux_ref[pl.ds(f, LINES, stride=8), :] = value
        flux_ref[pl.ds(f + NOUT, LINES, stride=8), :] = value


def soil_pass(theta, draw, level):
    above = jnp.where(level == 0, theta, pltpu.roll(theta, 1, 0))
    under = jnp.where(level == LEVELS - 1, theta, pltpu.roll(theta, theta.shape[0] - 1, 0))
    return theta + 0.25 * (above + under - 2.0 * theta) - draw


def drain(soil_ref, draw_ref, flux_ref):
    level = iota((8, 128), 0) + 8
    for j in range(LINES):
        lanes = slice(128 * j, 128 * (j + 1))
        draw = draw_ref[8:, lanes] * flux_ref[8 * j + 1 : 8 * j + 2, :]
        theta = jnp.concatenate([soil_ref[8:, lanes], jnp.zeros((1, 128), F32)], axis=0)
        for repeat in range(SOILP):
            theta = soil_pass(theta, draw, level)
        value = 0.5 * theta[LEVELS - 9 : LEVELS - 8, :]
        flux_ref[8 * j + 3 : 8 * j + 4, :] = value
        flux_ref[8 * j + 7 : 8 * j + 8, :] = value


def soil(soil_ref, draw_ref, field_ref, flux_ref):
    level = iota((16, 128), 0)
    for j in range(LINES):
        lanes = slice(128 * j, 128 * (j + 1))
        draw = draw_ref[:, lanes] * flux_ref[8 * j + 1 : 8 * j + 2, :]
        theta = jnp.concatenate([soil_ref[:, lanes], jnp.zeros((1, 128), F32)], axis=0)
        theta = theta + jnp.where(level == 0, 0.1 * field_ref[NF * j + 7 : NF * j + 8, :], 0.0)
        for repeat in range(SOILP):
            theta = soil_pass(theta, draw, level)
        soil_ref[:, lanes] = theta[:LEVELS]


def reply(flux_ref, quad_ref, p_ref, w_ref, msg_ref):
    line = iota((8, 128), 0)
    for j in range(LINES):
        flux = flux_ref[8 * j : 8 * (j + 1), :]
        quad = jnp.broadcast_to(quad_ref[j : j + 1, :], (8, 128))
        parts = [
            jnp.where((2 * k + line // NOUT).astype(F32) == quad, flux, 0.0) for k in range(QUADS // 2)
        ]
        w_ref[: NOUT * QUADS, 128 * j : 128 * (j + 1)] = jnp.concatenate(parts, axis=0).astype(BF16)
    held = []
    for w in range(3):
        mine = [c for c in range(CHUNKS) if window_of(c) == w]
        lanes = slice(mine[0] * STEP, (mine[-1] + 1) * STEP)
        held.append(dot_nt(p_ref[:, lanes], w_ref[: NOUT * QUADS, lanes]))
    parts = []
    for k in range(4):
        a, b, c = (g[WINDOW * k : WINDOW * (k + 1)] for g in held)
        rows = jnp.concatenate([a[:32], a[32:] + b[:32], b[32:] + c[:32], c[32:]], axis=0)
        rows = jnp.concatenate([rows, jnp.zeros((PEERS, 128 - NOUT * QUADS), F32)], axis=1)
        shift = NOUT * QUADS * k % 128
        parts.append(pltpu.roll(rows, shift, 1) if shift else rows)
    lane = iota((PEERS, 128), 1)
    lines = (
        jnp.where(lane < 80, parts[0], parts[1]),
        jnp.where(lane < 32, parts[1], jnp.where(lane < 112, parts[2], parts[3])),
        parts[3],
    )
    fold(lines, msg_ref)


def targets(column_ref, target_ref):
    ids = iota((BCOLS, 128), 0)
    for j in range(LINES):
        target_ref[:, 128 * j : 128 * (j + 1)] = as_bf16(ids == column_ref[j : j + 1, :])


def gather(home_ref, pair_ref, area_ref, split_ref, target_ref, atm_ref, both_ref):
    got = unfold(home_ref, BACK)
    rows = NOUT * QUADS
    part = lambda k: got[rows * k : rows * (k + 1), :]
    even = jnp.concatenate([part(0), part(2)], axis=0)
    odd = jnp.concatenate([part(1), part(3)], axis=0)
    lhs = jnp.concatenate([even, odd], axis=1).astype(BF16)
    line = iota((8, STEP), 0)
    for c in range(CHUNKS):
        g = dot(lhs, split_ref[:, c * STEP : (c + 1) * STEP])
        pair = jnp.broadcast_to(two_lines(pair_ref, c), (8, STEP))
        value = jnp.zeros((8, STEP), F32)
        for k in range(QUADS):
            label = 2 * (2 * (k % (QUADS // 2)) + line // NOUT) + k // (QUADS // 2)
            value = value + jnp.where(label.astype(F32) == pair, g[8 * k : 8 * (k + 1), :], 0.0)
        value = (value + pltpu.roll(value, NOUT, 0)) * two_lines(area_ref, c)
        high = value.astype(BF16).astype(F32)
        both_ref[:, c * STEP : (c + 1) * STEP] = jnp.where(line < NOUT, high, value - high)
    for b in range(ROWS // BROWS):
        lanes = slice(b * BROWS, (b + 1) * BROWS)
        total = dot_nt(both_ref[:, lanes].astype(BF16), target_ref[:, lanes])
        atm_ref[:, BCOLS * b : BCOLS * (b + 1)] = total[:NOUT] + total[NOUT:]


def step_kernel(
    owner_hbm, forcing_hbm, sunlit_hbm, type_hbm, leaf_hbm, soil_hbm, table_hbm, area_hbm, column_hbm,
    atm_ref, after_hbm,
    owner_ref, forcing_ref, sunlit_ref, type_ref, leaf_ref, soil_ref, table_ref, area_ref, column_ref,
    in_sem, out_sem, send_sem, recv_sem,
    msg_ref, got_ref, reply_ref, home_ref, flat_ref,
    pair_ref, quad_ref, a_ref, split_ref, w_ref, lhs_ref, p_ref, early_ref, draw_ref, field_ref, flux_ref,
    both_ref,
):
    copies = [
        pltpu.make_async_copy(a, b, in_sem.at[i])
        for i, (a, b) in enumerate(
            (
                (owner_hbm, owner_ref), (forcing_hbm, forcing_ref), (sunlit_hbm, sunlit_ref),
                (type_hbm, type_ref), (leaf_hbm, leaf_ref), (soil_hbm, soil_ref),
                (table_hbm, table_ref), (area_hbm, area_ref), (column_hbm, column_ref),
            )
        )
    ]
    for copy in copies:
        copy.start()
    here = place()
    greet(here)
    copies[0].wait()
    copies[1].wait()
    pack(owner_ref, forcing_ref, flat_ref, msg_ref, pair_ref, a_ref, split_ref, w_ref)
    pl.semaphore_wait(pltpu.get_barrier_semaphore(), PEERS - 1)
    send_all(here, msg_ref, got_ref, SENT, send_sem.at[0], recv_sem.at[0])
    for copy in copies[2:]:
        copy.wait()
    prepare(sunlit_ref, type_ref, leaf_ref, table_ref, early_ref, draw_ref)
    await_all(msg_ref, got_ref, SENT, send_sem.at[0], recv_sem.at[0])
    unpack(got_ref, flat_ref, lhs_ref, p_ref, quad_ref, field_ref)
    physics(early_ref, field_ref, flux_ref)
    drain(soil_ref, draw_ref, flux_ref)
    reply(flux_ref, quad_ref, p_ref, w_ref, reply_ref)
    send_all(here, reply_ref, home_ref, BACK, send_sem.at[1], recv_sem.at[1])
    soil(soil_ref, draw_ref, field_ref, flux_ref)
    after = pltpu.make_async_copy(soil_ref, after_hbm, out_sem)
    after.start()
    targets(column_ref, a_ref)
    await_all(reply_ref, home_ref, BACK, send_sem.at[1], recv_sem.at[1])
    gather(home_ref, pair_ref, area_ref, split_ref, a_ref, atm_ref, both_ref)
    after.wait()


def hand_on_kernel(atm_ref, after_ref, atm_out, after_out, atm_buf, after_buf, in_sem, out_sem):
    pairs = [(atm_ref, atm_buf, atm_out)]
    for i in range(PARTS):
        lanes = pl.ds(i * (ROWS // PARTS), ROWS // PARTS)
        pairs.append(tuple(ref.at[:, lanes] for ref in (after_ref, after_buf, after_out)))
    inward = [pltpu.make_async_copy(a, b, in_sem.at[i]) for i, (a, b, _) in enumerate(pairs)]
    outward = [pltpu.make_async_copy(b, c, out_sem.at[i]) for i, (_, b, c) in enumerate(pairs)]
    for copy in inward:
        copy.start()
    for one, two in zip(inward, outward):
        one.wait()
        two.start()
    for copy in outward:
        copy.wait()


def body(forcing, owner, column, area, sunlit, plant_type, leaf_area, soil_water, pft_table):
    lines = lambda x: x.reshape(LINES, 128)
    i32 = jnp.int32
    flat = lambda dtype: pltpu.VMEM((LINES, 128), dtype)
    there = pltpu.VMEM((PEERS, SENT + 1, 128), BF16)
    back = pltpu.VMEM((PEERS * 8 + 8, 128), F32)
    sem = pltpu.SemaphoreType.DMA
    atm_flux, soil_after = pl.pallas_call(
        step_kernel,
        out_shape=(
            jax.ShapeDtypeStruct((NOUT, ROWS // BROWS * BCOLS), F32),
            jax.ShapeDtypeStruct((LEVELS, ROWS), F32),
        ),
        in_specs=[pl.BlockSpec(memory_space=pl.ANY)] * 9,
        out_specs=(pl.BlockSpec(memory_space=pltpu.VMEM), pl.BlockSpec(memory_space=pl.ANY)),
        scratch_shapes=[
            flat(i32), pltpu.VMEM((NF, ROWS), BF16), flat(i32), flat(i32), flat(F32),
            pltpu.VMEM((LEVELS, ROWS), F32), pltpu.VMEM((4, NPFT), F32), flat(F32), flat(i32),
            sem((9,)), sem, sem((2,)), sem((2,)),
            there, there, back, back, back,
            flat(F32), flat(F32),
            pltpu.VMEM((PEERS, ROWS), BF16),
            pltpu.VMEM((2 * PEERS, ROWS), BF16),
            pltpu.VMEM((HALF + 16, ROWS), BF16),
            pltpu.VMEM((3, HALF // 2, STEP), BF16),
            pltpu.VMEM((4 * WINDOW, ROWS), BF16),
            pltpu.VMEM((6, LINES, 128), F32),
            pltpu.VMEM((16, ROWS), F32),
            pltpu.VMEM((LINES * NF + 8, 128), F32),
            pltpu.VMEM((LINES * 8 + 8, 128), F32),
            pltpu.VMEM((8, ROWS), F32),
        ],
        compiler_params=pltpu.CompilerParams(
            collective_id=1, has_side_effects=True, vmem_limit_bytes=VMEM_LIMIT
        ),
        name="step",
    )(
        lines(owner), forcing, lines(sunlit), lines(plant_type), lines(leaf_area), soil_water, pft_table,
        lines(area), lines(column),
    )
    return pl.pallas_call(
        hand_on_kernel,
        out_shape=(
            jax.ShapeDtypeStruct(atm_flux.shape, F32),
            jax.ShapeDtypeStruct(soil_after.shape, F32),
        ),
        in_specs=[pl.BlockSpec(memory_space=pl.ANY)] * 2,
        out_specs=(pl.BlockSpec(memory_space=pl.ANY),) * 2,
        scratch_shapes=[
            pltpu.VMEM(atm_flux.shape, F32), pltpu.VMEM(soil_after.shape, F32), sem((PARTS + 1,)), sem((PARTS + 1,)),
        ],
        compiler_params=pltpu.CompilerParams(vmem_limit_bytes=VMEM_LIMIT),
        name="hand_on",
    )(atm_flux, soil_after)


def solution(mesh):
    spec = P(("row", "col"))
    wide = P(None, ("row", "col"))
    return jax.shard_map(
        body,
        mesh=mesh,
        in_specs=(wide, spec, spec, spec, spec, spec, spec, wide, P()),
        out_specs=(wide, wide),
        check_vma=False,
    )
```

```python
import jax
import jax.numpy as jnp
from jax import lax
from jax.experimental import pallas as pl
from jax.experimental.pallas import tpu as pltpu
from jax.sharding import PartitionSpec as P

NF = 8
NOUT = 4
NPFT = 16
LEVELS = 15
ITERS = 4
SOILP = 4
BROWS = 512
BCOLS = 128
PEERS = 128
ROWS = 8192
LINES = ROWS // 128
SLOTS = 80
QUADS = SLOTS // 4
STEP = 256
CHUNKS = ROWS // STEP
HALF = 2 * QUADS * NF
WINDOW = 64
SENT = NF * SLOTS // 128
BACK = 3
PARTS = 4
MESH = pl.DeviceIdType.MESH
F32 = jnp.float32
BF16 = jnp.bfloat16
NT = (((1,), (1,)), ((), ()))
VMEM_LIMIT = 56 * 1024 * 1024


def iota(shape, dim):
    return lax.broadcasted_iota(jnp.int32, shape, dim)


def as_bf16(mask):
    return jnp.where(mask, 1.0, 0.0).astype(BF16)


def dot(a, b):
    return jnp.dot(a, b, preferred_element_type=F32)


def dot_nt(a, b):
    return lax.dot_general(a, b, NT, preferred_element_type=F32)


def times_row(hot, row):
    rows, width = hot.shape
    tile = jnp.broadcast_to(row, (16, width)).astype(BF16)
    return (hot.reshape(rows // 16, 16, width) * tile[None]).reshape(rows, width)


def two_lines(ref, c):
    return jnp.concatenate([ref[2 * c : 2 * c + 1, :], ref[2 * c + 1 : 2 * c + 2, :]], axis=1)


def hops(step):
    return min(step, 4 - step)


OFFSETS = sorted(
    [(y, k, x, z) for y in range(4) for k in range(2) for x in range(4) for z in range(4)][1:],
    key=lambda o: -(3 * (hops(o[0]) + hops(o[2]) + hops(o[3])) + o[1]),
)


def place():
    row, col = lax.axis_index("row"), lax.axis_index("col")
    return row // 2, lax.rem(row, 2), col // 4, lax.rem(col, 4)


def neighbour(here, offset):
    y, k, x, z = (lax.rem(a + b, n) for a, b, n in zip(here, offset, (4, 2, 4, 4)))
    return y * 2 + k, x * 4 + z


def greet(here):
    barrier = pltpu.get_barrier_semaphore()
    for offset in OFFSETS:
        pl.semaphore_signal(barrier, inc=1, device_id=neighbour(here, offset), device_id_type=MESH)


def slot_of(ref, index, lines):
    if ref.dtype == BF16:
        return ref.at[index]
    return ref.at[pl.ds(pl.multiple_of(index * 8, 8), lines), :]


def send_all(here, msg_ref, got_ref, lines, send_sem, recv_sem):
    row, col = neighbour(here, (0, 0, 0, 0))
    me = row * 16 + col
    for offset in OFFSETS:
        row, col = neighbour(here, offset)
        pltpu.make_async_remote_copy(
            src_ref=slot_of(msg_ref, row * 16 + col, lines),
            dst_ref=slot_of(got_ref, me, lines),
            send_sem=send_sem,
            recv_sem=recv_sem,
            device_id=(row, col),
            device_id_type=MESH,
        ).start()
    pltpu.make_async_copy(slot_of(msg_ref, me, lines), slot_of(got_ref, me, lines), recv_sem).start()


def await_all(msg_ref, got_ref, lines, send_sem, recv_sem):
    unit = 1 if msg_ref.dtype == BF16 else lines
    sent = msg_ref.at[: (PEERS - 1) * unit]
    pltpu.make_async_copy(sent, sent, send_sem).wait()
    got = got_ref.at[: PEERS * unit]
    pltpu.make_async_copy(got, got, recv_sem).wait()


def fold(lines, flat_ref):
    for i, line in enumerate(lines):
        flat_ref[pl.ds(i, PEERS, stride=8), :] = line


def unfold(flat_ref, lines):
    return jnp.concatenate([flat_ref[pl.ds(i, PEERS, stride=8), :].T for i in range(lines)], axis=0)


def pack(owner_ref, forcing_ref, flat_ref, msg_ref, pair_ref, a_ref, split_ref, w_ref):
    ids = iota((PEERS, 128), 0)
    for j in range(LINES):
        a_ref[:, 128 * j : 128 * (j + 1)] = as_bf16(ids == owner_ref[j : j + 1, :])
    upto = as_bf16(iota((STEP, STEP), 0) <= iota((STEP, STEP), 1))
    base = jnp.zeros((PEERS, 1), F32)
    for c in range(CHUNKS):
        a = a_ref[:, c * STEP : (c + 1) * STEP]
        seen = dot(a, upto)
        mine = (seen + base).astype(BF16) * a
        base = base + seen[:, STEP - 1 :]
        mine = mine.reshape(PEERS // 16, 16, STEP)
        total = mine[0]
        for i in range(1, PEERS // 16):
            total = total + mine[i]
        rank = jnp.sum(total.astype(F32), axis=0, keepdims=True) - 1.0
        pair = jnp.floor(rank * 0.5)
        odd = rank - 2.0 * pair
        pair_ref[2 * c : 2 * c + 1, :] = pair[:, :128]
        pair_ref[2 * c + 1 : 2 * c + 2, :] = pair[:, 128:]
        split_ref[:PEERS, c * STEP : (c + 1) * STEP] = times_row(a, 1.0 - odd)
        split_ref[PEERS:, c * STEP : (c + 1) * STEP] = times_row(a, odd)
    line = iota((16, STEP), 0)
    for c in range(CHUNKS):
        pair = jnp.broadcast_to(two_lines(pair_ref, c), (16, STEP)).astype(BF16)
        x = forcing_ref[:, c * STEP : (c + 1) * STEP].astype(F32)
        x = jnp.concatenate([x, x], axis=0).astype(BF16)
        for k in range(2 * QUADS // 2):
            label = 2 * (2 * (k % (QUADS // 2)) + line // 8) + k // (QUADS // 2)
            hit = label.astype(F32).astype(BF16) == pair
            w_ref[16 * k : 16 * (k + 1), c * STEP : (c + 1) * STEP] = jnp.where(hit, x, jnp.zeros((), BF16))
    w_ref[HALF:, :] = jnp.ones((16, ROWS), BF16)
    got = dot_nt(w_ref[...], split_ref[...])
    counts = got[HALF : HALF + 1, :PEERS] + got[HALF : HALF + 1, PEERS:]
    line = iota((HALF, PEERS), 0)
    label = 4 * (lax.rem(line, HALF // 2) // NF) + 2 * (line // (HALF // 2))
    values = [
        jnp.where((label + odd).astype(F32) < counts, got[:HALF, PEERS * odd : PEERS * (odd + 1)], -1.0)
        for odd in range(2)
    ]
    values = jnp.concatenate(values, axis=0)
    lines = [values[128 * i : 128 * (i + 1), :].T for i in range(SENT)]
    fold(lines + [jnp.zeros((PEERS, 128), F32)], flat_ref)
    msg_ref[...] = flat_ref[: PEERS * 8, :].reshape(PEERS, 8, 128)[:, : SENT + 1].astype(BF16)


def look(row, kinds):
    return jnp.take_along_axis(jnp.broadcast_to(row, kinds.shape), kinds, axis=1, mode="promise_in_bounds")


def prepare(sunlit_ref, type_ref, leaf_ref, table_ref, early_ref, draw_ref):
    table = jnp.concatenate([table_ref[...], jnp.zeros((4, 128 - NPFT), F32)], axis=1)
    single_t = jnp.sqrt(1.0 - (0.1 + 0.3 * table[0:1]))
    reflect_t = (1.0 - single_t) / (1.0 + single_t)
    kroot_t = 0.05 + 0.5 * table[3:4]
    level = iota((16, 128), 0)
    roots_t = jnp.where(level < LEVELS, jnp.exp(-kroot_t * level.astype(F32)), 0.0)
    roots_t = 0.05 * (roots_t / jnp.sum(roots_t, axis=0, keepdims=True))
    kinds = type_ref[...]
    leaf = leaf_ref[...]
    single = look(single_t, kinds)
    reflect_h = look(reflect_t, kinds)
    lit = sunlit_ref[...].astype(F32)
    early_ref[0] = single * leaf
    early_ref[1] = reflect_h
    early_ref[2] = look(0.5 + 1.5 * table[1:2], kinds)
    early_ref[3] = look(3.0 + 6.0 * table[2:3], kinds)
    early_ref[4] = lit
    early_ref[5] = lit * (1.0 - reflect_h) * (1.0 - jnp.exp(-0.8 * single * leaf))
    for j in range(LINES):
        draw_ref[:, 128 * j : 128 * (j + 1)] = look(roots_t, jnp.broadcast_to(type_ref[j : j + 1, :], (16, 128)))


def window_of(c):
    least = c * STEP // SLOTS
    most = min(PEERS - 1, (PEERS * SLOTS - ROWS + c * STEP + STEP - 1) // SLOTS)
    for w in range(3):
        if 32 * w <= least and most < 32 * w + WINDOW:
            return w
    raise ValueError


def arrange(got_ref, flat_ref, lhs_ref):
    got = jnp.concatenate([got_ref[...].astype(F32), jnp.zeros((PEERS, 2, 128), F32)], axis=1)
    flat_ref[: PEERS * 8, :] = got.reshape(PEERS * 8, 128)
    got = unfold(flat_ref, SENT)
    valid = jnp.where(got >= 0.0, 1.0 / NF, 0.0)
    counts = jnp.sum(valid, axis=0, keepdims=True)
    part = lambda odd, a: got[HALF * odd + HALF // 2 * a : HALF * odd + HALF // 2 * (a + 1), :]
    low = iota((HALF // 2, 128), 1) < WINDOW
    for a in range(2):
        even, odd = part(0, a), part(1, a)
        for w in range(3):
            left = even if w == 0 else pltpu.roll(even, 128 - 32 * w, 1)
            right = odd if w == 2 else pltpu.roll(odd, 64 - 32 * w, 1)
            lhs_ref[w, :, 128 * a : 128 * (a + 1)] = jnp.where(low, left, right).astype(BF16)
    before = iota((PEERS, PEERS), 1) < iota((PEERS, PEERS), 0)
    upto = iota((PEERS, PEERS), 1) <= iota((PEERS, PEERS), 0)
    ones = jnp.ones((PEERS, STEP), BF16)
    begin = dot(jnp.where(before, counts, 0.0).astype(BF16), ones)
    end = dot(jnp.where(upto, counts, 0.0).astype(BF16), ones)
    return begin, end


def unpack(got_ref, flat_ref, lhs_ref, p_ref, quad_ref, field_ref):
    begin, end = arrange(got_ref, flat_ref, lhs_ref)
    for c in range(CHUNKS):
        w = window_of(c)
        first = begin[32 * w : 32 * w + WINDOW]
        tile = (iota((1, STEP), 1) + c * STEP).astype(F32)
        mine = (tile >= first) & (tile < end[32 * w : 32 * w + WINDOW])
        slot = tile - jnp.sum(jnp.where(mine, first, 0.0), axis=0, keepdims=True)
        quad = jnp.floor(slot * 0.25)
        rest = slot - 4.0 * quad
        quad_ref[2 * c : 2 * c + 1, :] = quad[:, :128]
        quad_ref[2 * c + 1 : 2 * c + 2, :] = quad[:, 128:]
        hot = as_bf16(mine)
        for k in range(4):
            p_ref[WINDOW * k : WINDOW * (k + 1), c * STEP : (c + 1) * STEP] = times_row(
                hot, jnp.where(rest == float(k), 1.0, 0.0)
            )
    for c in range(CHUNKS):
        g = dot(lhs_ref[window_of(c)], p_ref[:, c * STEP : (c + 1) * STEP])
        quad = jnp.broadcast_to(two_lines(quad_ref, c), (NF, STEP))
        value = jnp.zeros((NF, STEP), F32)
        for s in range(QUADS):
            value = value + jnp.where(quad == float(s), g[NF * s : NF * (s + 1), :], 0.0)
        field_ref[NF * 2 * c : NF * (2 * c + 1), :] = value[:, :128]
        field_ref[NF * (2 * c + 1) : NF * (2 * c + 2), :] = value[:, 128:]


def physics(early_ref, field_ref, flux_ref):
    field = lambda f: field_ref[pl.ds(f, LINES, stride=NF), :]
    thick, reflect_h, vcmax, slope, lit, diffuse = (early_ref[i] for i in range(6))
    swdir = 2.0 * field(0)
    tair = field(2) - 0.5
    vapour = 0.2 + field(3)
    carbon = 0.8 + 0.4 * field(4)
    coszen = 0.1 + 0.9 * field(5)
    wind_speed = 0.5 + 2.0 * field(6)
    extinct = 0.5 / coszen
    reflect_b = 2.0 * extinct * reflect_h / (1.0 + extinct)
    light = lit * (1.0 - reflect_b) * swdir * (1.0 - jnp.exp(-extinct * thick)) + diffuse * field(1)
    electrons = 0.3 * light
    compensation = 0.08 * (1.0 + 0.3 * tair)
    capacity_t = vcmax * jnp.exp(0.5 * tair)
    internal = 0.7 * carbon
    for repeat in range(ITERS):
        limit = internal - compensation
        carboxyl = capacity_t * limit / (internal + 0.6)
        ribulose = electrons * limit / (4.0 * internal + 8.0 * compensation)
        assim = carboxyl * ribulose / (carboxyl + ribulose)
        conduct = 0.05 + slope * assim / carbon
        internal = carbon - 1.6 * assim / conduct
    transpire = conduct * vapour
    for f, value in enumerate((assim, transpire, 0.5 * wind_speed * (0.2 * light - 0.5 * transpire))):
        flux_ref[pl.ds(f, LINES, stride=8), :] = value
        flux_ref[pl.ds(f + NOUT, LINES, stride=8), :] = value


def soil_pass(theta, draw, level):
    above = jnp.where(level == 0, theta, pltpu.roll(theta, 1, 0))
    under = jnp.where(level == LEVELS - 1, theta, pltpu.roll(theta, theta.shape[0] - 1, 0))
    return theta + 0.25 * (above + under - 2.0 * theta) - draw


def drain(soil_ref, draw_ref, flux_ref):
    level = iota((8, 128), 0) + 8
    for j in range(LINES):
        lanes = slice(128 * j, 128 * (j + 1))
        draw = draw_ref[8:, lanes] * flux_ref[8 * j + 1 : 8 * j + 2, :]
        theta = jnp.concatenate([soil_ref[8:, lanes], jnp.zeros((1, 128), F32)], axis=0)
        for repeat in range(SOILP):
            theta = soil_pass(theta, draw, level)
        value = 0.5 * theta[LEVELS - 9 : LEVELS - 8, :]
        flux_ref[8 * j + 3 : 8 * j + 4, :] = value
        flux_ref[8 * j + 7 : 8 * j + 8, :] = value


def soil(soil_ref, draw_ref, field_ref, flux_ref):
    level = iota((16, 128), 0)
    for j in range(LINES):
        lanes = slice(128 * j, 128 * (j + 1))
        draw = draw_ref[:, lanes] * flux_ref[8 * j + 1 : 8 * j + 2, :]
        theta = jnp.concatenate([soil_ref[:, lanes], jnp.zeros((1, 128), F32)], axis=0)
        theta = theta + jnp.where(level == 0, 0.1 * field_ref[NF * j + 7 : NF * j + 8, :], 0.0)
        for repeat in range(SOILP):
            theta = soil_pass(theta, draw, level)
        soil_ref[:, lanes] = theta[:LEVELS]


def reply(flux_ref, quad_ref, p_ref, w_ref, msg_ref):
    line = iota((8, 128), 0)
    for j in range(LINES):
        flux = flux_ref[8 * j : 8 * (j + 1), :]
        quad = jnp.broadcast_to(quad_ref[j : j + 1, :], (8, 128))
        parts = [
            jnp.where((2 * k + line // NOUT).astype(F32) == quad, flux, 0.0) for k in range(QUADS // 2)
        ]
        w_ref[: NOUT * QUADS, 128 * j : 128 * (j + 1)] = jnp.concatenate(parts, axis=0).astype(BF16)
    held = []
    for w in range(3):
        mine = [c for c in range(CHUNKS) if window_of(c) == w]
        lanes = slice(mine[0] * STEP, (mine[-1] + 1) * STEP)
        held.append(dot_nt(p_ref[:, lanes], w_ref[: NOUT * QUADS, lanes]))
    parts = []
    for k in range(4):
        a, b, c = (g[WINDOW * k : WINDOW * (k + 1)] for g in held)
        rows = jnp.concatenate([a[:32], a[32:] + b[:32], b[32:] + c[:32], c[32:]], axis=0)
        rows = jnp.concatenate([rows, jnp.zeros((PEERS, 128 - NOUT * QUADS), F32)], axis=1)
        shift = NOUT * QUADS * k % 128
        parts.append(pltpu.roll(rows, shift, 1) if shift else rows)
    lane = iota((PEERS, 128), 1)
    lines = (
        jnp.where(lane < 80, parts[0], parts[1]),
        jnp.where(lane < 32, parts[1], jnp.where(lane < 112, parts[2], parts[3])),
        parts[3],
    )
    fold(lines, msg_ref)


def targets(column_ref, target_ref):
    ids = iota((BCOLS, 128), 0)
    for j in range(LINES):
        target_ref[:, 128 * j : 128 * (j + 1)] = as_bf16(ids == column_ref[j : j + 1, :])


def gather(home_ref, pair_ref, area_ref, split_ref, target_ref, atm_ref, both_ref, halves):
    got = unfold(home_ref, BACK)
    rows = NOUT * QUADS
    part = lambda k: got[rows * k : rows * (k + 1), :]
    even = jnp.concatenate([part(0), part(2)], axis=0)
    odd = jnp.concatenate([part(1), part(3)], axis=0)
    lhs = jnp.concatenate([even, odd], axis=1).astype(BF16)
    line = iota((8, STEP), 0)
    for c in range(CHUNKS):
        g = dot(lhs, split_ref[:, c * STEP : (c + 1) * STEP])
        pair = jnp.broadcast_to(two_lines(pair_ref, c), (8, STEP))
        value = jnp.zeros((8, STEP), F32)
        for k in range(QUADS):
            label = 2 * (2 * (k % (QUADS // 2)) + line // NOUT) + k // (QUADS // 2)
            value = value + jnp.where(label.astype(F32) == pair, g[8 * k : 8 * (k + 1), :], 0.0)
        value = (value + pltpu.roll(value, NOUT, 0)) * two_lines(area_ref, c)
        high = value.astype(BF16).astype(F32)
        both_ref[:, c * STEP : (c + 1) * STEP] = jnp.where(line < NOUT, high, value - high)
    for b in range(ROWS // BROWS):
        lanes = slice(b * BROWS, (b + 1) * BROWS)
        total = dot_nt(both_ref[:, lanes].astype(BF16), target_ref[:, lanes])
        atm_ref[b // 8, :, BCOLS * (b % 8) : BCOLS * (b % 8 + 1)] = total[:NOUT] + total[NOUT:]
        if b % 8 == 7:
            halves[b // 8].start()


def step_kernel(
    owner_hbm, forcing_hbm, sunlit_hbm, type_hbm, leaf_hbm, soil_hbm, table_hbm, area_hbm, column_hbm,
    atm_hbm, after_hbm,
    owner_ref, forcing_ref, sunlit_ref, type_ref, leaf_ref, soil_ref, table_ref, area_ref, column_ref,
    in_sem, out_sem, send_sem, recv_sem,
    msg_ref, got_ref, reply_ref, home_ref, flat_ref,
    pair_ref, quad_ref, a_ref, split_ref, w_ref, lhs_ref, p_ref, early_ref, draw_ref, field_ref, flux_ref,
    both_ref, atm_ref,
):
    copies = [
        pltpu.make_async_copy(a, b, in_sem.at[i])
        for i, (a, b) in enumerate(
            (
                (owner_hbm, owner_ref), (forcing_hbm, forcing_ref), (sunlit_hbm, sunlit_ref),
                (type_hbm, type_ref), (leaf_hbm, leaf_ref), (soil_hbm, soil_ref),
                (table_hbm, table_ref), (area_hbm, area_ref), (column_hbm, column_ref),
            )
        )
    ]
    for copy in copies:
        copy.start()
    here = place()
    greet(here)
    copies[0].wait()
    copies[1].wait()
    pack(owner_ref, forcing_ref, flat_ref, msg_ref, pair_ref, a_ref, split_ref, w_ref)
    pl.semaphore_wait(pltpu.get_barrier_semaphore(), PEERS - 1)
    send_all(here, msg_ref, got_ref, SENT, send_sem.at[0], recv_sem.at[0])
    for copy in copies[2:]:
        copy.wait()
    prepare(sunlit_ref, type_ref, leaf_ref, table_ref, early_ref, draw_ref)
    await_all(msg_ref, got_ref, SENT, send_sem.at[0], recv_sem.at[0])
    unpack(got_ref, flat_ref, lhs_ref, p_ref, quad_ref, field_ref)
    physics(early_ref, field_ref, flux_ref)
    drain(soil_ref, draw_ref, flux_ref)
    reply(flux_ref, quad_ref, p_ref, w_ref, reply_ref)
    send_all(here, reply_ref, home_ref, BACK, send_sem.at[1], recv_sem.at[1])
    soil(soil_ref, draw_ref, field_ref, flux_ref)
    half = ROWS // BROWS * BCOLS // 2
    halves = [
        pltpu.make_async_copy(atm_ref.at[i], atm_hbm.at[:, pl.ds(i * half, half)], out_sem.at[i + 1]) for i in range(2)
    ]
    after = pltpu.make_async_copy(soil_ref, after_hbm, out_sem.at[0])
    after.start()
    targets(column_ref, a_ref)
    await_all(reply_ref, home_ref, BACK, send_sem.at[1], recv_sem.at[1])
    gather(home_ref, pair_ref, area_ref, split_ref, a_ref, atm_ref, both_ref, halves)
    for copy in halves:
        copy.wait()
    after.wait()


def hand_on_kernel(atm_ref, after_ref, atm_out, after_out, atm_buf, after_buf, in_sem, out_sem):
    pairs = [(atm_ref, atm_buf, atm_out)]
    for i in range(PARTS):
        lanes = pl.ds(i * (ROWS // PARTS), ROWS // PARTS)
        pairs.append(tuple(ref.at[:, lanes] for ref in (after_ref, after_buf, after_out)))
    inward = [pltpu.make_async_copy(a, b, in_sem.at[i]) for i, (a, b, _) in enumerate(pairs)]
    outward = [pltpu.make_async_copy(b, c, out_sem.at[i]) for i, (_, b, c) in enumerate(pairs)]
    for copy in inward:
        copy.start()
    for one, two in zip(inward, outward):
        one.wait()
        two.start()
    for copy in outward:
        copy.wait()


def body(forcing, owner, column, area, sunlit, plant_type, leaf_area, soil_water, pft_table):
    lines = lambda x: x.reshape(LINES, 128)
    i32 = jnp.int32
    flat = lambda dtype: pltpu.VMEM((LINES, 128), dtype)
    there = pltpu.VMEM((PEERS, SENT + 1, 128), BF16)
    back = pltpu.VMEM((PEERS * 8 + 8, 128), F32)
    sem = pltpu.SemaphoreType.DMA
    atm_flux, soil_after = pl.pallas_call(
        step_kernel,
        out_shape=(
            jax.ShapeDtypeStruct((NOUT, ROWS // BROWS * BCOLS), F32),
            jax.ShapeDtypeStruct((LEVELS, ROWS), F32),
        ),
        in_specs=[pl.BlockSpec(memory_space=pl.ANY)] * 9,
        out_specs=(pl.BlockSpec(memory_space=pl.ANY),) * 2,
        scratch_shapes=[
            flat(i32), pltpu.VMEM((NF, ROWS), BF16), flat(i32), flat(i32), flat(F32),
            pltpu.VMEM((LEVELS, ROWS), F32), pltpu.VMEM((4, NPFT), F32), flat(F32), flat(i32),
            sem((9,)), sem((3,)), sem((2,)), sem((2,)),
            there, there, back, back, back,
            flat(F32), flat(F32),
            pltpu.VMEM((PEERS, ROWS), BF16),
            pltpu.VMEM((2 * PEERS, ROWS), BF16),
            pltpu.VMEM((HALF + 16, ROWS), BF16),
            pltpu.VMEM((3, HALF // 2, STEP), BF16),
            pltpu.VMEM((4 * WINDOW, ROWS), BF16),
            pltpu.VMEM((6, LINES, 128), F32),
            pltpu.VMEM((16, ROWS), F32),
            pltpu.VMEM((LINES * NF + 8, 128), F32),
            pltpu.VMEM((LINES * 8 + 8, 128), F32),
            pltpu.VMEM((8, ROWS), F32),
            pltpu.VMEM((2, NOUT, ROWS // BROWS * BCOLS // 2), F32),
        ],
        compiler_params=pltpu.CompilerParams(
            collective_id=1, has_side_effects=True, vmem_limit_bytes=VMEM_LIMIT
        ),
        name="step",
    )(
        lines(owner), forcing, lines(sunlit), lines(plant_type), lines(leaf_area), soil_water, pft_table,
        lines(area), lines(column),
    )
    return pl.pallas_call(
        hand_on_kernel,
        out_shape=(
            jax.ShapeDtypeStruct(atm_flux.shape, F32),
            jax.ShapeDtypeStruct(soil_after.shape, F32),
        ),
        in_specs=[pl.BlockSpec(memory_space=pl.ANY)] * 2,
        out_specs=(pl.BlockSpec(memory_space=pl.ANY),) * 2,
        scratch_shapes=[
            pltpu.VMEM(atm_flux.shape, F32), pltpu.VMEM(soil_after.shape, F32), sem((PARTS + 1,)), sem((PARTS + 1,)),
        ],
        compiler_params=pltpu.CompilerParams(vmem_limit_bytes=VMEM_LIMIT),
        name="hand_on",
    )(atm_flux, soil_after)


def solution(mesh):
    spec = P(("row", "col"))
    wide = P(None, ("row", "col"))
    return jax.shard_map(
        body,
        mesh=mesh,
        in_specs=(wide, spec, spec, spec, spec, spec, spec, wide, P()),
        out_specs=(wide, wide),
        check_vma=False,
    )
```
